256 devices in a mesh: clip: 64 (over z, y, core), space: 2 (over x_hi), tm: 2 (over x_lo).
Axes of the slice: x: 4 (x_hi: 2, x_lo: 2; x = x_hi * 2 + x_lo), y: 4, z: 8, core: 2. Of those that a mesh axis runs over, the one named last changes fastest.
Arguments:
- gen_latent: bfloat16 [64, 4, 8, 128, 16], P('clip', 'tm', 'space'), may hold values from -6 to 6
- frame_counts: int32 [64], replicated, may hold values from 1 to 4, as said below
- owner_map: int32 [64], replicated, may hold values from 0 to 63, as said below
- w_in: bfloat16 [3, 3, 16, 512], replicated, may hold values from -0.5 to 0.5
- w_query: bfloat16 [512, 512], replicated
- w_key: bfloat16 [512, 512], replicated, may hold values from -0.25 to 0.25
- w_value: bfloat16 [512, 512], replicated, may hold values from -0.25 to 0.25
- w_out: bfloat16 [512, 512], replicated, may hold values from -0.25 to 0.25
- w_space: bfloat16 [3, 3, 512, 512], replicated, may hold values from -0.09375 to 0.09375
- w_time: bfloat16 [3, 512, 512], replicated, may hold values from -0.15625 to 0.15625
- w_head: bfloat16 [512, 12], replicated, may hold values from -0.25 to 0.25
Outputs:
- pixels: float32 [64, 4, 3, 16, 256], P('clip', 'tm', None, 'space')
The draws below stay inside these ranges and needn't reach their ends.
Inputs may be any that keep to these rules, and one draw needn't show every extreme that they name: `frame_counts`: some clip has all 4 frames live. `owner_map`: each decoder slot is named once; some generator clip g goes to decoder slot (g + 32) mod 64.
All inputs are finite; a program needn't handle non-finite values.
Results may differ from the reference program's by a relative error of at most 0.027.
Values may be sent and summed in bfloat16 or wider, within the bound.
A program may use at most 64 MiB of HBM per device.

```python
import math
import jax
import jax.numpy as jnp
from jax import lax

CH = 512
LAT_CH = 16
HEAD = 12
W = 128
CLIPS = 64
T_LAT = 4
H = 8


def draw_frame_counts(key, part):
    key = jax.random.fold_in(key, 11)
    first_key, second_key = jax.random.split(key)
    counts = jax.random.randint(first_key, (CLIPS,), 1, T_LAT + 1)
    chosen = jax.random.randint(second_key, (), 0, CLIPS)
    return counts.at[chosen].set(T_LAT).astype(jnp.int32)


def draw_owner_map(key, part):
    key = jax.random.fold_in(key, 13)
    first_key, second_key = jax.random.split(key)
    order = jax.random.permutation(first_key, CLIPS).astype(jnp.int32)
    chosen = jax.random.randint(second_key, (), 0, CLIPS).astype(jnp.int32)
    target = (chosen + CLIPS // 2) % CLIPS
    holder = jnp.argmax((order == target).astype(jnp.int32)).astype(jnp.int32)
    previous = order[chosen]
    order = order.at[holder].set(previous)
    order = order.at[chosen].set(target)
    return order.astype(jnp.int32)


def draw_w_query(key, part):
    key = jax.random.fold_in(key, 12)
    matrix = jax.random.normal(key, (CH, CH), jnp.float32) * CH ** (-0.5)
    return matrix.astype(jnp.bfloat16)


def levels(key, shape, shards, least, top_value):
    def one(position, blocks):
        heights = jax.random.uniform(jax.random.fold_in(jax.random.fold_in(key, 6), position), (blocks,), jnp.float32, least / len(shards), top_value / len(shards))
        return jnp.repeat(jnp.exp(heights), shape[position] // blocks).reshape((-1,) + (1,) * (len(shape) - position - 1))

    loudness = one(*shards[0])
    for cut in shards[1:]:
        loudness = loudness * one(*cut)
    return loudness


def normal_values(own_key, shape, scale, bound, pieces=(), kind=jnp.bfloat16):
    array = jax.random.normal(own_key, shape, jnp.float32) * scale
    if len(pieces) > 0:
        array = levels(own_key, shape, pieces, -0.22, 0.18) * array
    return jnp.clip(array, min=-bound, max=bound).astype(kind)


def setup_inputs(seed: int = 0) -> dict:
    splits = jax.random.split(jax.random.key(seed), 12)
    gen_latent = normal_values(splits[0], (CLIPS, T_LAT, H, W, LAT_CH), 1.0, 6.0, ((0, 64), (1, 2), (2, 2)))
    frame_counts = draw_frame_counts(jax.random.fold_in(splits[11], 71), 0)
    owner_map = draw_owner_map(jax.random.fold_in(splits[11], 71), 0)
    w_in = normal_values(splits[3], (3, 3, LAT_CH, CH), (9 * LAT_CH) ** -0.5, 0.5)
    w_query = draw_w_query(jax.random.fold_in(splits[11], 71), 0)
    w_key = normal_values(splits[5], (CH, CH), CH ** -0.5, 0.25)
    w_value = normal_values(splits[6], (CH, CH), CH ** -0.5, 0.25)
    w_out = normal_values(splits[7], (CH, CH), CH ** -0.5, 0.25)
    w_space = normal_values(splits[8], (3, 3, CH, CH), (9 * CH) ** -0.5, 0.09375)
    w_time = normal_values(splits[9], (3, CH, CH), (3 * CH) ** -0.5, 0.15625)
    w_head = normal_values(splits[10], (CH, HEAD), CH ** -0.5, 0.25)
    return {"gen_latent": gen_latent, "frame_counts": frame_counts, "owner_map": owner_map, "w_in": w_in, "w_query": w_query, "w_key": w_key, "w_value": w_value, "w_out": w_out, "w_space": w_space, "w_time": w_time, "w_head": w_head}


EPS = 1e-06

def normed(field):
    wide = field.astype(jnp.float32)
    return wide * lax.rsqrt(lax.optimization_barrier(jnp.mean(wide * wide, axis=-1, keepdims=True)) + EPS)

def spatial_conv(padded, weight):
    height = padded.shape[-3] - 2
    width = padded.shape[-2]
    side_pad = jnp.pad(padded, [(0, 0)] * (padded.ndim - 2) + [(1, 1), (0, 0)])
    result = None
    for row_step in range(3):
        for col_step in range(3):
            window = side_pad[..., row_step:row_step + height, col_step:col_step + width, :]
            term = jnp.dot(window, weight[row_step, col_step], preferred_element_type=jnp.float32)
            result = term if result is None else result + term
    return result

def inverse_haar(coeffs):
    lead = coeffs.shape[:-3]
    height, width = (coeffs.shape[-3], coeffs.shape[-2])
    low_low = coeffs[..., 0:3]
    low_high = coeffs[..., 3:6]
    high_low = coeffs[..., 6:9]
    high_high = coeffs[..., 9:12]
    even_even = (low_low + low_high + high_low + high_high) * 0.5
    even_odd = (low_low - low_high + high_low - high_high) * 0.5
    odd_even = (low_low + low_high - high_low - high_high) * 0.5
    odd_odd = (low_low - low_high - high_low + high_high) * 0.5
    upper = jnp.stack([even_even, even_odd], axis=-2).reshape(lead + (height, 2 * width, 3))
    lower = jnp.stack([odd_even, odd_odd], axis=-2).reshape(lead + (height, 2 * width, 3))
    joined = jnp.stack([upper, lower], axis=-3).reshape(lead + (2 * height, 2 * width, 3))
    return jnp.moveaxis(joined, -1, -3)

def reference(gen_latent, frame_counts, owner_map, w_in, w_query, w_key, w_value, w_out, w_space, w_time, w_head):
    inverse = jnp.zeros((CLIPS,), jnp.int32).at[owner_map].set(jnp.arange(CLIPS, dtype=jnp.int32))
    latent = gen_latent[inverse]
    live_all = frame_counts[inverse]
    frames = jnp.arange(T_LAT, dtype=jnp.int32)
    causal = (frames[:, None] >= frames[None, :])[:, None, None, :]

    def decode(item):
        latent_clip, live = item
        padded = jnp.pad(latent_clip, ((0, 0), (1, 1), (0, 0), (0, 0)))
        first = spatial_conv(padded, w_in).astype(jnp.bfloat16)
        normal_in = normed(first).astype(jnp.bfloat16)
        queries = jnp.dot(normal_in, w_query, preferred_element_type=jnp.float32).astype(jnp.bfloat16)
        keys = jnp.dot(normal_in, w_key, preferred_element_type=jnp.float32).astype(jnp.bfloat16)
        values = jnp.dot(normal_in, w_value, preferred_element_type=jnp.float32).astype(jnp.bfloat16)
        scores = jnp.einsum('thwd,shwd->thws', queries.astype(jnp.float32), keys.astype(jnp.float32)) / math.sqrt(CH)
        masked = jnp.where(causal, scores, jnp.float32(-1e+30))
        highest = lax.optimization_barrier(jnp.max(masked, axis=-1, keepdims=True))
        weights = jnp.where(causal, jnp.exp(masked - highest), jnp.float32(0.0))
        total = lax.optimization_barrier(jnp.sum(weights, axis=-1))
        rounded = weights.astype(jnp.bfloat16)
        mixed = jnp.einsum('thws,shwd->thwd', rounded.astype(jnp.float32), values.astype(jnp.float32))
        attended = (mixed / total[..., None]).astype(jnp.bfloat16)
        second = (first.astype(jnp.float32) + jnp.dot(attended, w_out, preferred_element_type=jnp.float32)).astype(jnp.bfloat16)
        activated = jax.nn.silu(normed(second)).astype(jnp.bfloat16)
        spread = spatial_conv(jnp.pad(activated, ((0, 0), (1, 1), (0, 0), (0, 0))), w_space).astype(jnp.bfloat16)
        extended = jnp.concatenate([jnp.zeros((2,) + spread.shape[1:], jnp.bfloat16), spread], axis=0)
        temporal = None
        for offset in range(3):
            term = jnp.dot(extended[offset:offset + T_LAT], w_time[offset], preferred_element_type=jnp.float32)
            temporal = term if temporal is None else temporal + term
        third = (second.astype(jnp.float32) + temporal).astype(jnp.bfloat16)
        coeffs = jnp.dot(third, w_head, preferred_element_type=jnp.float32)
        image = inverse_haar(coeffs)
        keep = (frames < live).astype(jnp.float32)
        return image * keep[:, None, None, None]
    return lax.map(decode, (latent, live_all))
```

```python
import functools
import math

import jax
import jax.numpy as jnp
from jax import lax
from jax.experimental import pallas as pl
from jax.experimental.pallas import tpu as pltpu
from jax.sharding import PartitionSpec as P

EPS = 1e-06
MESH = pl.DeviceIdType.MESH
F32 = jnp.float32
BF16 = jnp.bfloat16
WIDE = 128
PAIR = 2 * WIDE


def dot(a, b):
    return jnp.dot(a, b, preferred_element_type=F32)


def dot_nt(a, b):
    return lax.dot_general(a, b, (((1,), (1,)), ((), ())), preferred_element_type=F32)


def kernel(
    plane,
    planes,
    owner,
    counts,
    lat,
    w_in,
    w_query,
    w_key,
    w_value,
    w_out,
    w_space,
    w_time,
    w_head,
    out,
    v_in,
    v_query,
    v_key,
    v_value,
    v_out,
    v_space,
    v_time,
    v_head,
    in_t,
    head16,
    qk_t,
    vo_t,
    taps,
    eff,
    spread_cols,
    gat_a,
    gat_b,
    p_buf,
    got_a,
    got_b,
    quarter,
    panel,
    patches,
    first,
    normal,
    query,
    mixed,
    active,
    head_sum,
    parts,
    total,
    total16,
    from_tm,
    from_edge,
    owned,
    pixel_rows,
    w_sem,
    own_sem,
    g_send,
    g_recv,
    p_send,
    p_recv,
    x_send,
    x_recv,
    o_send,
    o_recv,
):
    ch = v_query.shape[0]
    me = lax.axis_index("clip")
    s = lax.axis_index("space")
    t = lax.axis_index("tm")
    m = lax.rem(me, plane)
    z = me // plane
    base = z * plane
    gat = (gat_a, gat_b)
    got = (got_a, got_b)

    loads = [
        pltpu.make_async_copy(src, dst, w_sem.at[i])
        for i, (src, dst) in enumerate(
            (
                (w_key, v_key),
                (w_query, v_query),
                (w_value, v_value),
                (w_out, v_out),
                (w_head, v_head),
                (w_in, v_in),
                (w_time, v_time),
                (w_space, v_space),
            )
        )
    ]
    l_key, l_query, l_value, l_out, l_head, l_in, l_time, l_space = loads

    def plane_peer(d):
        return (base + lax.rem(m + d, plane), s, t)

    def column_peer(d):
        return (lax.rem(z + d, planes) * plane + m, s, t)

    x_peers = [(me, s, 1 - t), (me, 1 - s, t), (me, 1 - s, 1 - t)]
    everyone = [plane_peer(d) for d in range(1, plane)]
    everyone += [column_peer(d) for d in range(1, planes)] + x_peers
    barrier = pltpu.get_barrier_semaphore()
    for peer in everyone:
        pl.semaphore_signal(barrier, inc=1, device_id=peer, device_id_type=MESH)
    ways = ((planes, column_peer, z), (plane, plane_peer, m))
    own = [
        pltpu.make_async_copy(lat.at[c], gat[c].at[ways[c][2]], own_sem.at[c]) for c in range(2)
    ]
    for copy in own + loads:
        copy.start()
    pl.semaphore_wait(barrier, len(everyone))

    gathers = ([], [])
    for c in range(2):
        count, peer, place = ways[c]
        for d in sorted(range(1, count), key=lambda d: -min(d, count - d)):
            copy = pltpu.make_async_remote_copy(
                src_ref=lat.at[c],
                dst_ref=gat[c].at[place],
                send_sem=g_send.at[c, d],
                recv_sem=g_recv.at[c, d],
                device_id=peer(d),
                device_id_type=MESH,
            )
            copy.start()
            gathers[c].append(copy)

    picks = ([], [])
    for d in range(plane):
        slot = base + lax.rem(m + d, plane)
        pick = jnp.int32(0)
        for i in range(planes):
            pick = jnp.where(owner[i * plane + m] == slot, jnp.int32(i), pick)
        picks[0].append(pick)
    for d in range(planes):
        slot = lax.rem(z + d, planes) * plane + m
        pick = jnp.int32(0)
        for i in range(plane):
            pick = jnp.where(owner[base + i] == slot, jnp.int32(i), pick)
        picks[1].append(pick)

    def scan(g, carry):
        from_a, from_b, live = carry
        here = owner[g] == me
        step_a = lax.rem(m - lax.rem(g, plane) + plane, plane)
        step_b = lax.rem(z - g // plane + planes, planes)
        return (
            jnp.where(here, step_a, from_a),
            jnp.where(here, step_b, from_b),
            jnp.where(here, counts[g], live),
        )

    from_a, from_b, live = lax.fori_loop(0, plane * planes, scan, (jnp.int32(0),) * 3)

    l_key.wait()
    l_query.wait()
    qk_t[...] = dot_nt(v_key[...], v_query[...]).astype(BF16)
    l_value.wait()
    l_out.wait()
    vo_t[0:ch, :] = dot(v_value[...], v_out[...]).T.astype(BF16)

    passes = []
    for c in (1, 0):
        count, peer, _ = ways[1 - c]
        own[c].wait()
        for copy in gathers[c]:
            copy.wait_recv()
        for d in sorted(range(count), key=lambda d: -min(d, count - d)):
            block = gat[c][picks[c][d]]
            if d == 0:
                got[c][0] = block
                continue
            p_buf[c, d] = block
            copy = pltpu.make_async_remote_copy(
                src_ref=p_buf.at[c, d],
                dst_ref=got[c].at[d],
                send_sem=p_send.at[c, d],
                recv_sem=p_recv.at[c, d],
                device_id=peer(d),
                device_id_type=MESH,
            )
            copy.start()
            passes.append(copy)

    l_head.wait()
    wide = v_head[...].astype(F32)
    gap = jnp.zeros((1, ch), F32)
    head16[...] = jnp.concatenate(
        [wide[0:3], gap, wide[3:6], gap, wide[6:9], gap, wide[9:12], gap], axis=0
    ).astype(BF16)
    l_in.wait()
    in_t[0:ch, :] = v_in[...].astype(F32).T.astype(BF16)
    in_t[ch : ch + 16, :] = dot_nt(head16[...], v_in[...]).astype(BF16)
    vo_t[ch : ch + 16, :] = dot(head16[...], vo_t[0:ch, :]).astype(BF16)
    l_time.wait()
    for k in range(3):
        taps[16 * k : 16 * k + 16, :] = dot_nt(head16[...], v_time[k]).astype(BF16)
    l_space.wait()

    def fold(i, carry):
        eff[i] = dot_nt(taps[...], v_space[i]).astype(BF16)
        return carry

    lax.fori_loop(0, 6, fold, 0)

    for copy in passes:
        copy.wait_recv()
    quarter[0] = got_a[from_a]
    quarter[1] = got_b[from_b]

    def exchange(i, src, dst, peer, sems):
        copy = pltpu.make_async_remote_copy(
            src_ref=src,
            dst_ref=dst,
            send_sem=sems[0].at[i],
            recv_sem=sems[1].at[i],
            device_id=peer,
            device_id_type=MESH,
        )
        copy.start()
        return copy

    frames = pl.ds(2 * t, 2)
    sems = (x_send, x_recv)
    rows = [
        exchange(0, quarter.at[:, pl.ds(1 - t, 3)], panel.at[frames, pl.ds(t, 3)], x_peers[0], sems),
        exchange(1, quarter.at[:, 3 * (1 - s)], panel.at[frames, 3 * t], x_peers[1], sems),
        exchange(2, quarter.at[:, 3 * (1 - s)], panel.at[frames, 3 * (1 - t)], x_peers[2], sems),
    ]
    for f in range(2):
        for r in range(3):
            panel[2 * t + f, 1 - t + r] = quarter[f, t + r]

    lax.fori_loop(6, 9, fold, 0)
    r_id = lax.broadcasted_iota(jnp.int32, (PAIR, PAIR), 0)
    c_id = lax.broadcasted_iota(jnp.int32, (PAIR, PAIR), 1)
    goal = jnp.where(r_id < WIDE, 2 * r_id, 2 * (r_id - WIDE) + 1)
    spread_cols[...] = jnp.where(goal == c_id, 1.0, 0.0).astype(BF16)
    parts[...] = jnp.zeros(parts.shape, F32)

    for copy in rows:
        copy.wait_recv()

    lane = lax.broadcasted_iota(jnp.int32, (16, WIDE), 1)
    top = jnp.logical_not(jnp.logical_and(s == 0, t == 0))
    bottom = jnp.logical_not(jnp.logical_and(s == 1, t == 1))
    for f in range(4):
        for r in range(4):
            tile = panel[f, r].astype(F32)
            if r == 0:
                tile = jnp.where(top, tile, 0.0)
            if r == 3:
                tile = jnp.where(bottom, tile, 0.0)
            left = jnp.where(lane == 0, 0.0, pltpu.roll(tile, 1, 1))
            right = jnp.where(lane == WIDE - 1, 0.0, pltpu.roll(tile, WIDE - 1, 1))
            for b, value in enumerate((left, tile, right)):
                value = value.astype(BF16)
                for a in range(3):
                    row = r - a
                    if row in (0, 1):
                        start = 16 * (3 * a + b)
                        patches[f, start : start + 16, row * WIDE : (row + 1) * WIDE] = value

    def inverse_rms(square):
        return lax.rsqrt(jnp.sum(square, axis=0, keepdims=True) / ch + EPS)

    tiles = [slice(c, c + 16) for c in range(0, ch, 16)]

    for f in range(4):
        wide = dot(in_t[...], patches[f])
        head_sum[f] = wide[ch : ch + 16]
        square = jnp.zeros((16, PAIR), F32)
        for c in tiles:
            x = wide[c]
            first[f, c, :] = x
            square = square + x * x
        scale = inverse_rms(square)
        for c in tiles:
            normal[f, c, :] = (first[f, c, :] * scale).astype(BF16)

    def make_query(f):
        query[f] = dot(qk_t[...], normal[f]).astype(BF16)

    def attend(f):
        accs = [jnp.zeros((16, PAIR), F32)] * (f + 1)
        for c in range(0, ch, 64):
            for g in range(f + 1):
                p = [
                    query[f, i : i + 16, :] * normal[g, i : i + 16, :]
                    for i in range(c, c + 64, 16)
                ]
                accs[g] = accs[g] + ((p[0] + p[1]) + (p[2] + p[3])).astype(F32)
        scores = [jnp.sum(acc, axis=0, keepdims=True) * (1.0 / math.sqrt(ch)) for acc in accs]
        highest = functools.reduce(jnp.maximum, scores)
        weights = [jnp.exp(x - highest) for x in scores]
        norm = 1.0 / functools.reduce(jnp.add, weights)
        weights = [jnp.broadcast_to(w * norm, (16, PAIR)).astype(BF16) for w in weights]
        for c in tiles:
            mixed[f, c, :] = functools.reduce(
                jnp.add, [w * normal[g, c, :] for g, w in enumerate(weights)]
            )

    def activate(f):
        wide = dot(vo_t[...], mixed[f])
        head = head_sum[f] + wide[ch : ch + 16]
        for row in range(2):
            spot = (1, f, row + 1)
            parts[spot] = parts[spot] + head[:, row * WIDE : (row + 1) * WIDE]
        square = jnp.zeros((16, PAIR), F32)
        for c in tiles:
            x = first[f, c, :] + wide[c]
            first[f, c, :] = x
            square = square + x * x
        scale = inverse_rms(square) * 0.5
        for c in tiles:
            x = first[f, c, :] * scale
            active[f, c, :] = (x + x * jnp.tanh(x)).astype(BF16)

    def spread(f):
        wide = dot(eff[...].reshape(432, ch), active[f])
        for a in range(3):
            for b in range(3):
                for k in range(3):
                    start = 16 * (9 * a + 3 * b + k)
                    for row in range(2):
                        here = slice(row * WIDE, (row + 1) * WIDE)
                        spot = (b, f + 2 - k, row + 2 - a)
                        parts[spot] = parts[spot] + wide[start : start + 16, here]

    make_query(0)
    for f in range(4):
        if f < 3:
            make_query(f + 1)
        attend(f)
        activate(f)
        if f > 0:
            spread(f - 1)
    spread(3)

    for f in range(4):
        for r in range(4):
            left = jnp.where(lane == 0, 0.0, pltpu.roll(parts[0, f, r], 1, 1))
            right = jnp.where(lane == WIDE - 1, 0.0, pltpu.roll(parts[2, f, r], WIDE - 1, 1))
            value = parts[1, f, r] + left + right
            total[f, r] = value
            total16[f, r] = value.astype(BF16)

    sems = (o_send, o_recv)
    coeffs = [
        exchange(0, total16.at[pl.ds(2 * (1 - t), 2), pl.ds(1 - t, 3)], from_tm, x_peers[0], sems),
        exchange(1, total16.at[frames, 3 * t], from_edge.at[0], x_peers[1], sems),
        exchange(2, total16.at[pl.ds(2 * (1 - t), 2), 3 * t], from_edge.at[1], x_peers[2], sems),
    ]
    owned[...] = jnp.zeros(owned.shape, F32)
    for f in range(2):
        for r in range(3):
            owned[f, t + r] = total[2 * t + f, 1 - t + r]
    for copy in coeffs:
        copy.wait_recv()
    which = jnp.where(s == t, 0, 1)
    for f in range(2):
        for r in range(3):
            owned[f, 1 - t + r] = owned[f, 1 - t + r] + from_tm[f, r].astype(F32)
        edge = from_edge[which, f].astype(F32)
        owned[f, 3 * (1 - s)] = owned[f, 3 * (1 - s)] + edge

    for f in range(2):
        for h in range(4):
            low, high = owned[f, h, 0:8, :], owned[f, h, 8:16, :]
            for i, value in enumerate((low + high, low - high)):
                at = pl.ds(32 * f + 2 * h + i, 4, stride=8)
                pixel_rows[0, at, :] = (value[0:4] + value[4:8]) * 0.5
                pixel_rows[1, at, :] = (value[0:4] - value[4:8]) * 0.5
    both = jnp.concatenate([pixel_rows[0], pixel_rows[1]], axis=1)
    big = both.astype(BF16)
    small = (both - big.astype(F32)).astype(BF16)
    image = dot(big, spread_cols[...]) + dot(small, spread_cols[...])
    for f in range(2):
        keep = jnp.where(2 * t + f < live, 1.0, 0.0).astype(F32)
        for colour in range(3):
            start = 32 * f + 8 * colour
            out[0, f, colour] = image[start : start + 8] * keep

    for row in gathers:
        for copy in row:
            copy.wait_send()
    for copy in passes + rows + coeffs:
        copy.wait_send()


def solution(mesh):
    clips = mesh.shape["clip"]
    plane = 1 << (clips.bit_length() // 2)
    planes = clips // plane
    most = max(plane, planes)

    def body(
        gen_latent,
        frame_counts,
        owner_map,
        w_in,
        w_query,
        w_key,
        w_value,
        w_out,
        w_space,
        w_time,
        w_head,
    ):
        ch = w_query.shape[0]
        lat = jnp.swapaxes(gen_latent, -1, -2)[0]
        flat_in = w_in.reshape(144, ch)
        flat_space = w_space.reshape(9, ch, ch)
        vm = pltpu.VMEM
        dma = pltpu.SemaphoreType.DMA
        scratch = [
            vm((144, ch), BF16),
            vm((ch, ch), BF16),
            vm((ch, ch), BF16),
            vm((ch, ch), BF16),
            vm((ch, ch), BF16),
            vm((9, ch, ch), BF16),
            vm((3, ch, ch), BF16),
            vm((12, ch), BF16),
            vm((ch + 16, 144), BF16),
            vm((16, ch), BF16),
            vm((ch, ch), BF16),
            vm((ch + 16, ch), BF16),
            vm((48, ch), BF16),
            vm((9, 48, ch), BF16),
            vm((PAIR, PAIR), BF16),
            vm((planes, 4, 16, WIDE), BF16),
            vm((plane, 4, 16, WIDE), BF16),
            vm((2, most, 4, 16, WIDE), BF16),
            vm((plane, 4, 16, WIDE), BF16),
            vm((planes, 4, 16, WIDE), BF16),
            vm((2, 4, 16, WIDE), BF16),
            vm((4, 4, 16, WIDE), BF16),
            vm((4, 144, PAIR), BF16),
            vm((4, ch, PAIR), F32),
            vm((4, ch, PAIR), BF16),
            vm((4, ch, PAIR), BF16),
            vm((4, ch, PAIR), BF16),
            vm((4, ch, PAIR), BF16),
            vm((4, 16, PAIR), F32),
            vm((3, 6, 4, 16, WIDE), F32),
            vm((4, 4, 16, WIDE), F32),
            vm((4, 4, 16, WIDE), BF16),
            vm((2, 3, 16, WIDE), BF16),
            vm((2, 2, 16, WIDE), BF16),
            vm((2, 4, 16, WIDE), F32),
            vm((2, 64, WIDE), F32),
            dma((8,)),
            dma((2,)),
            dma((2, most)),
            dma((2, most)),
            dma((2, most)),
            dma((2, most)),
            dma((3,)),
            dma((3,)),
            dma((3,)),
            dma((3,)),
        ]
        hbm = pl.BlockSpec(memory_space=pltpu.HBM)
        smem = pl.BlockSpec(memory_space=pltpu.SMEM)
        return pl.pallas_call(
            functools.partial(kernel, plane, planes),
            out_shape=jax.ShapeDtypeStruct((1, 2, 3, 8, 2 * WIDE), F32),
            in_specs=[smem, smem] + [hbm] * 9,
            out_specs=pl.BlockSpec(memory_space=pltpu.VMEM),
            scratch_shapes=scratch,
            compiler_params=pltpu.CompilerParams(
                collective_id=0, has_side_effects=True, vmem_limit_bytes=64 * 1024 * 1024 - 65536
            ),
        )(
            owner_map,
            frame_counts,
            lat,
            flat_in,
            w_query,
            w_key,
            w_value,
            w_out,
            flat_space,
            w_time,
            w_head.T,
        )

    return jax.shard_map(
        body,
        mesh=mesh,
        in_specs=(P("clip", "tm", "space", None, None),) + (P(),) * 10,
        out_specs=P("clip", "tm", None, "space", None),
        check_vma=False,
    )
```

```python
import functools
import math

import jax
import jax.numpy as jnp
from jax import lax
from jax.experimental import pallas as pl
from jax.experimental.pallas import tpu as pltpu
from jax.sharding import PartitionSpec as P

EPS = 1e-06
MESH = pl.DeviceIdType.MESH
F32 = jnp.float32
BF16 = jnp.bfloat16
WIDE = 128
PAIR = 2 * WIDE


def dot(a, b):
    return jnp.dot(a, b, preferred_element_type=F32)


def dot_nt(a, b):
    return lax.dot_general(a, b, (((1,), (1,)), ((), ())), preferred_element_type=F32)


def kernel(
    plane,
    planes,
    owner,
    counts,
    lat,
    w_in,
    w_query,
    w_key,
    w_value,
    w_out,
    w_space,
    w_time,
    w_head,
    out,
    v_in,
    v_query,
    v_key,
    v_value,
    v_out,
    v_space,
    v_time,
    v_head,
    in_t,
    head16,
    qk_t,
    vo_t,
    taps,
    eff,
    spread_cols,
    gat_a,
    gat_b,
    p_buf,
    got_a,
    got_b,
    quarter,
    panel,
    patches,
    first,
    normal,
    query,
    mixed,
    active,
    head_sum,
    parts,
    to_tm,
    to_edge,
    from_tm,
    from_edge,
    owned,
    pixel_rows,
    w_sem,
    own_sem,
    g_send,
    g_recv,
    p_send,
    p_recv,
    x_send,
    x_recv,
    o_send,
    o_recv,
):
    ch = v_query.shape[0]
    me = lax.axis_index("clip")
    s = lax.axis_index("space")
    t = lax.axis_index("tm")
    m = lax.rem(me, plane)
    z = me // plane
    base = z * plane
    gat = (gat_a, gat_b)
    got = (got_a, got_b)

    loads = [
        pltpu.make_async_copy(src, dst, w_sem.at[i])
        for i, (src, dst) in enumerate(
            (
                (w_key, v_key),
                (w_query, v_query),
                (w_value, v_value),
                (w_out, v_out),
                (w_head, v_head),
                (w_in, v_in),
                (w_time, v_time),
                (w_space, v_space),
            )
        )
    ]
    l_key, l_query, l_value, l_out, l_head, l_in, l_time, l_space = loads

    def plane_peer(d):
        return (base + lax.rem(m + d, plane), s, t)

    def column_peer(d):
        return (lax.rem(z + d, planes) * plane + m, s, t)

    x_peers = [(me, s, 1 - t), (me, 1 - s, t), (me, 1 - s, 1 - t)]
    everyone = [plane_peer(d) for d in range(1, plane)]
    everyone += [column_peer(d) for d in range(1, planes)] + x_peers
    barrier = pltpu.get_barrier_semaphore()
    for peer in everyone:
        pl.semaphore_signal(barrier, inc=1, device_id=peer, device_id_type=MESH)
    ways = ((planes, column_peer, z), (plane, plane_peer, m))
    own = [
        pltpu.make_async_copy(lat.at[c], gat[c].at[ways[c][2]], own_sem.at[c]) for c in range(2)
    ]
    for copy in own + loads:
        copy.start()
    picks = ([], [])
    for d in range(plane):
        slot = base + lax.rem(m + d, plane)
        pick = jnp.int32(0)
        for i in range(planes):
            pick = jnp.where(owner[i * plane + m] == slot, jnp.int32(i), pick)
        picks[0].append(pick)
    for d in range(planes):
        slot = lax.rem(z + d, planes) * plane + m
        pick = jnp.int32(0)
        for i in range(plane):
            pick = jnp.where(owner[base + i] == slot, jnp.int32(i), pick)
        picks[1].append(pick)

    def products():
        l_key.wait()
        l_query.wait()
        qk_t[...] = dot_nt(v_key[...], v_query[...]).astype(BF16)
        l_value.wait()
        l_out.wait()
        vo_t[0:ch, :] = dot(v_value[...], v_out[...]).T.astype(BF16)
        l_head.wait()
        wide = v_head[...].astype(F32)
        gap = jnp.zeros((1, ch), F32)
        head16[...] = jnp.concatenate(
            [wide[0:3], gap, wide[3:6], gap, wide[6:9], gap, wide[9:12], gap], axis=0
        ).astype(BF16)
        l_time.wait()
        for k in range(3):
            taps[16 * k : 16 * k + 16, :] = dot_nt(head16[...], v_time[2 - k]).astype(BF16)

        l_in.wait()
        in_t[0:ch, :] = v_in[...].astype(F32).T.astype(BF16)
        in_t[ch : ch + 16, :] = dot_nt(head16[...], v_in[...]).astype(BF16)
        vo_t[ch : ch + 16, :] = dot(head16[...], vo_t[0:ch, :]).astype(BF16)
        l_space.wait()

        def fold(i):
            got = dot_nt(taps[...], v_space[i]).astype(BF16)
            for k in range(3):
                eff[k, i] = got[16 * k : 16 * k + 16]

        for i in range(9):
            fold(i)

        r_id = lax.broadcasted_iota(jnp.int32, (PAIR, PAIR), 0)
        c_id = lax.broadcasted_iota(jnp.int32, (PAIR, PAIR), 1)
        goal = jnp.where(r_id < WIDE, 2 * r_id, 2 * (r_id - WIDE) + 1)
        spread_cols[...] = jnp.where(goal == c_id, 1.0, 0.0).astype(BF16)
        parts[...] = jnp.zeros(parts.shape, F32)

    early = z + lax.rem(m, 2) + m // 2 < planes // 2
    pl.when(early)(products)

    for copy in own:
        copy.wait()
    pl.semaphore_wait(barrier, len(everyone))

    gathers = ([], [])
    for c in range(2):
        count, peer, place = ways[c]
        for d in sorted(range(1, count), key=lambda d: -min(d, count - d)):
            copy = pltpu.make_async_remote_copy(
                src_ref=gat[c].at[place],
                dst_ref=gat[c].at[place],
                send_sem=g_send.at[c, d],
                recv_sem=g_recv.at[c, d],
                device_id=peer(d),
                device_id_type=MESH,
            )
            copy.start()
            gathers[c].append(copy)

    passes = []
    for c in (1, 0):
        count, peer, _ = ways[1 - c]
        for copy in gathers[c]:
            copy.wait_recv()
        for d in sorted(range(count), key=lambda d: -min(d, count - d)):
            block = gat[c][picks[c][d]]
            if d == 0:
                got[c][0] = block
                continue
            p_buf[c, d] = block
            copy = pltpu.make_async_remote_copy(
                src_ref=p_buf.at[c, d],
                dst_ref=got[c].at[d],
                send_sem=p_send.at[c, d],
                recv_sem=p_recv.at[c, d],
                device_id=peer(d),
                device_id_type=MESH,
            )
            copy.start()
            passes.append(copy)

    def scan(g, carry):
        from_a, from_b, live = carry
        here = owner[g] == me
        step_a = lax.rem(m - lax.rem(g, plane) + plane, plane)
        step_b = lax.rem(z - g // plane + planes, planes)
        return (
            jnp.where(here, step_a, from_a),
            jnp.where(here, step_b, from_b),
            jnp.where(here, counts[g], live),
        )

    from_a, from_b, live = lax.fori_loop(0, plane * planes, scan, (jnp.int32(0),) * 3, unroll=8)

    pl.when(jnp.logical_not(early))(products)

    for copy in passes:
        copy.wait_recv()
    quarter[0] = got_a[from_a]
    quarter[1] = got_b[from_b]

    def exchange(i, src, dst, peer, sems):
        copy = pltpu.make_async_remote_copy(
            src_ref=src,
            dst_ref=dst,
            send_sem=sems[0].at[i],
            recv_sem=sems[1].at[i],
            device_id=peer,
            device_id_type=MESH,
        )
        copy.start()
        return copy

    frames = pl.ds(2 * t, 2)
    sems = (x_send, x_recv)
    rows = [
        exchange(0, quarter.at[:, pl.ds(1 - t, 3)], panel.at[frames, pl.ds(t, 3)], x_peers[0], sems),
        exchange(1, quarter.at[:, 3 * (1 - s)], panel.at[frames, 3 * t], x_peers[1], sems),
        exchange(2, quarter.at[:, 3 * (1 - s)], panel.at[frames, 3 * (1 - t)], x_peers[2], sems),
    ]
    for f in range(2):
        for r in range(3):
            panel[2 * t + f, 1 - t + r] = quarter[f, t + r]

    for copy in rows:
        copy.wait_recv()

    lane = lax.broadcasted_iota(jnp.int32, (16, WIDE), 1)
    top = jnp.logical_not(jnp.logical_and(s == 0, t == 0))
    bottom = jnp.logical_not(jnp.logical_and(s == 1, t == 1))
    for f in range(4):
        for r in range(4):
            tile = panel[f, r].astype(F32)
            if r == 0:
                tile = jnp.where(top, tile, 0.0)
            if r == 3:
                tile = jnp.where(bottom, tile, 0.0)
            left = jnp.where(lane == 0, 0.0, pltpu.roll(tile, 1, 1))
            right = jnp.where(lane == WIDE - 1, 0.0, pltpu.roll(tile, WIDE - 1, 1))
            for b, value in enumerate((left, tile, right)):
                value = value.astype(BF16)
                for a in range(3):
                    row = r - a
                    if row in (0, 1):
                        start = 16 * (3 * a + b)
                        patches[f, start : start + 16, row * WIDE : (row + 1) * WIDE] = value

    def inverse_rms(square):
        return lax.rsqrt(jnp.sum(square, axis=0, keepdims=True) / ch + EPS)

    tiles = [slice(c, c + 16) for c in range(0, ch, 16)]

    for f in range(4):
        wide = dot(in_t[...], patches[f])
        head_sum[f] = wide[ch : ch + 16]
        square = jnp.zeros((16, PAIR), F32)
        for c in tiles:
            x = wide[c]
            first[f, c, :] = x
            square = square + x * x
        scale = inverse_rms(square)
        for c in tiles:
            normal[f, c, :] = (first[f, c, :] * scale).astype(BF16)

    def make_query(f):
        query[f] = dot(qk_t[...], normal[f]).astype(BF16)

    def attend(f):
        accs = [jnp.zeros((16, PAIR), F32)] * (f + 1)
        for c in range(0, ch, 64):
            for g in range(f + 1):
                p = [
                    query[f, i : i + 16, :] * normal[g, i : i + 16, :]
                    for i in range(c, c + 64, 16)
                ]
                accs[g] = accs[g] + ((p[0] + p[1]) + (p[2] + p[3])).astype(F32)
        scores = [jnp.sum(acc, axis=0, keepdims=True) * (1.0 / math.sqrt(ch)) for acc in accs]
        highest = functools.reduce(jnp.maximum, scores)
        weights = [jnp.exp(x - highest) for x in scores]
        norm = 1.0 / functools.reduce(jnp.add, weights)
        weights = [jnp.broadcast_to(w * norm, (16, PAIR)).astype(BF16) for w in weights]
        for c in tiles:
            mixed[f, c, :] = functools.reduce(
                jnp.add, [w * normal[g, c, :] for g, w in enumerate(weights)]
            )

    def activate(f):
        wide = dot(vo_t[...], mixed[f])
        head = head_sum[f] + wide[ch : ch + 16]
        for row in range(2):
            spot = (f, row + 1)
            parts[spot] = parts[spot] + head[:, row * WIDE : (row + 1) * WIDE]
        square = jnp.zeros((16, PAIR), F32)
        for c in tiles:
            x = first[f, c, :] + wide[c]
            first[f, c, :] = x
            square = square + x * x
        scale = inverse_rms(square) * 0.5
        for c in tiles:
            x = first[f, c, :] * scale
            active[f, c, :] = (x + x * jnp.tanh(x)).astype(BF16)

    def spread(f):
        steps = min(3, 4 - f)
        wide = dot(eff[0:steps].reshape(144 * steps, ch), active[f])
        for k in range(steps):
            for r in range(4):
                sides = []
                for b in range(3):
                    pieces = []
                    for row in range(2):
                        a = row + 2 - r
                        if 0 <= a < 3:
                            start = 144 * k + 16 * (3 * a + b)
                            here = slice(row * WIDE, (row + 1) * WIDE)
                            pieces.append(wide[start : start + 16, here])
                    sides.append(functools.reduce(jnp.add, pieces))
                left = jnp.where(lane == 0, 0.0, pltpu.roll(sides[0], 1, 1))
                right = jnp.where(lane == WIDE - 1, 0.0, pltpu.roll(sides[2], WIDE - 1, 1))
                parts[f + k, r] = parts[f + k, r] + (sides[1] + (left + right))

    make_query(0)
    for f in range(4):
        if f < 3:
            make_query(f + 1)
        attend(f)
        activate(f)
        if f > 0:
            spread(f - 1)
    spread(3)

    for f in range(2):
        for r in range(3):
            to_tm[f, r] = parts[2 * (1 - t) + f, 1 - t + r].astype(BF16)
    for f in range(4):
        to_edge[f] = parts[f, 3 * t].astype(BF16)
    sems = (o_send, o_recv)
    coeffs = [
        exchange(0, to_tm, from_tm, x_peers[0], sems),
        exchange(1, to_edge.at[frames], from_edge.at[0], x_peers[1], sems),
        exchange(2, to_edge.at[pl.ds(2 * (1 - t), 2)], from_edge.at[1], x_peers[2], sems),
    ]
    owned[...] = jnp.zeros(owned.shape, F32)
    for f in range(2):
        for r in range(3):
            owned[f, t + r] = parts[2 * t + f, 1 - t + r]
    for copy in coeffs:
        copy.wait_recv()
    which = jnp.where(s == t, 0, 1)
    for f in range(2):
        for r in range(3):
            owned[f, 1 - t + r] = owned[f, 1 - t + r] + from_tm[f, r].astype(F32)
        edge = from_edge[which, f].astype(F32)
        owned[f, 3 * (1 - s)] = owned[f, 3 * (1 - s)] + edge

    for f in range(2):
        for h in range(4):
            low, high = owned[f, h, 0:8, :], owned[f, h, 8:16, :]
            for i, value in enumerate((low + high, low - high)):
                at = pl.ds(32 * f + 2 * h + i, 4, stride=8)
                pixel_rows[0, at, :] = (value[0:4] + value[4:8]) * 0.5
                pixel_rows[1, at, :] = (value[0:4] - value[4:8]) * 0.5
    both = jnp.concatenate([pixel_rows[0], pixel_rows[1]], axis=1)
    big = both.astype(BF16)
    small = (both - big.astype(F32)).astype(BF16)
    image = dot(big, spread_cols[...]) + dot(small, spread_cols[...])
    for f in range(2):
        keep = jnp.where(2 * t + f < live, 1.0, 0.0).astype(F32)
        for colour in range(3):
            start = 32 * f + 8 * colour
            out[0, f, colour] = image[start : start + 8] * keep

    for row in gathers:
        for copy in row:
            copy.wait_send()
    for copy in passes + rows + coeffs:
        copy.wait_send()


def solution(mesh):
    clips = mesh.shape["clip"]
    plane = 1 << (clips.bit_length() // 2)
    planes = clips // plane
    most = max(plane, planes)

    def body(
        gen_latent,
        frame_counts,
        owner_map,
        w_in,
        w_query,
        w_key,
        w_value,
        w_out,
        w_space,
        w_time,
        w_head,
    ):
        ch = w_query.shape[0]
        lat = jnp.swapaxes(gen_latent, -1, -2)[0]
        flat_in = w_in.reshape(144, ch)
        flat_space = w_space.reshape(9, ch, ch)
        vm = pltpu.VMEM
        dma = pltpu.SemaphoreType.DMA
        scratch = [
            vm((144, ch), BF16),
            vm((ch, ch), BF16),
            vm((ch, ch), BF16),
            vm((ch, ch), BF16),
            vm((ch, ch), BF16),
            vm((9, ch, ch), BF16),
            vm((3, ch, ch), BF16),
            vm((12, ch), BF16),
            vm((ch + 16, 144), BF16),
            vm((16, ch), BF16),
            vm((ch, ch), BF16),
            vm((ch + 16, ch), BF16),
            vm((48, ch), BF16),
            vm((3, 9, 16, ch), BF16),
            vm((PAIR, PAIR), BF16),
            vm((planes, 4, 16, WIDE), BF16),
            vm((plane, 4, 16, WIDE), BF16),
            vm((2, most, 4, 16, WIDE), BF16),
            vm((plane, 4, 16, WIDE), BF16),
            vm((planes, 4, 16, WIDE), BF16),
            vm((2, 4, 16, WIDE), BF16),
            vm((4, 4, 16, WIDE), BF16),
            vm((4, 144, PAIR), BF16),
            vm((4, ch, PAIR), F32),
            vm((4, ch, PAIR), BF16),
            vm((4, ch, PAIR), BF16),
            vm((4, ch, PAIR), BF16),
            vm((4, ch, PAIR), BF16),
            vm((4, 16, PAIR), F32),
            vm((4, 4, 16, WIDE), F32),
            vm((2, 3, 16, WIDE), BF16),
            vm((4, 16, WIDE), BF16),
            vm((2, 3, 16, WIDE), BF16),
            vm((2, 2, 16, WIDE), BF16),
            vm((2, 4, 16, WIDE), F32),
            vm((2, 64, WIDE), F32),
            dma((8,)),
            dma((2,)),
            dma((2, most)),
            dma((2, most)),
            dma((2, most)),
            dma((2, most)),
            dma((3,)),
            dma((3,)),
            dma((3,)),
            dma((3,)),
        ]
        hbm = pl.BlockSpec(memory_space=pltpu.HBM)
        smem = pl.BlockSpec(memory_space=pltpu.SMEM)
        return pl.pallas_call(
            functools.partial(kernel, plane, planes),
            out_shape=pltpu.VMEM((1, 2, 3, 8, 2 * WIDE), F32),
            in_specs=[smem, smem] + [hbm] * 9,
            out_specs=pl.BlockSpec(memory_space=pltpu.VMEM),
            scratch_shapes=scratch,
            compiler_params=pltpu.CompilerParams(
                collective_id=0, has_side_effects=True, vmem_limit_bytes=62 * 1024 * 1024
            ),
        )(
            owner_map,
            frame_counts,
            lat,
            flat_in,
            w_query,
            w_key,
            w_value,
            w_out,
            flat_space,
            w_time,
            w_head.T,
        )

    return jax.shard_map(
        body,
        mesh=mesh,
        in_specs=(P("clip", "tm", "space", None, None),) + (P(),) * 10,
        out_specs=P("clip", "tm", None, "space", None),
        check_vma=False,
    )
```

```python
import functools
import math

import jax
import jax.numpy as jnp
from jax import lax
from jax.experimental import pallas as pl
from jax.experimental.pallas import tpu as pltpu
from jax.sharding import PartitionSpec as P

EPS = 1e-06
MESH = pl.DeviceIdType.MESH
F32 = jnp.float32
BF16 = jnp.bfloat16
WIDE = 128
PAIR = 2 * WIDE


def dot(a, b):
    return jnp.dot(a, b, preferred_element_type=F32)


def dot_nt(a, b):
    return lax.dot_general(a, b, (((1,), (1,)), ((), ())), preferred_element_type=F32)


def kernel(
    plane,
    planes,
    owner_hbm,
    counts_hbm,
    lat,
    w_in,
    w_query,
    w_key,
    w_value,
    w_out,
    w_space,
    w_time,
    w_head,
    out,
    v_in,
    v_query,
    v_key,
    v_value,
    v_out,
    v_space,
    v_time,
    v_head,
    owner,
    counts,
    in_t,
    head16,
    qk_t,
    vo_t,
    taps,
    eff,
    spread_cols,
    gat_a,
    gat_b,
    p_buf,
    got_a,
    got_b,
    quarter,
    panel,
    patches,
    first,
    normal,
    query,
    mixed,
    active,
    head_sum,
    parts,
    to_tm,
    to_edge,
    from_tm,
    from_edge,
    owned,
    pixel_rows,
    w_sem,
    own_sem,
    g_send,
    g_recv,
    p_send,
    p_recv,
    x_send,
    x_recv,
    o_send,
    o_recv,
):
    ch = v_query.shape[0]
    me = lax.axis_index("clip")
    s = lax.axis_index("space")
    t = lax.axis_index("tm")
    m = lax.rem(me, plane)
    z = me // plane
    base = z * plane
    gat = (gat_a, gat_b)
    got = (got_a, got_b)

    loads = [
        pltpu.make_async_copy(src, dst, w_sem.at[i])
        for i, (src, dst) in enumerate(
            (
                (w_key, v_key),
                (w_query, v_query),
                (w_value, v_value),
                (w_out, v_out),
                (w_head, v_head),
                (w_in, v_in),
                (w_time, v_time),
                (w_space, v_space),
            )
        )
    ]
    l_key, l_query, l_value, l_out, l_head, l_in, l_time, l_space = loads

    def plane_peer(d):
        return (base + lax.rem(m + d, plane), s, t)

    def column_peer(d):
        return (lax.rem(z + d, planes) * plane + m, s, t)

    x_peers = [(me, s, 1 - t), (me, 1 - s, t), (me, 1 - s, 1 - t)]
    everyone = [plane_peer(d) for d in range(1, plane)]
    everyone += [column_peer(d) for d in range(1, planes)] + x_peers
    barrier = pltpu.get_barrier_semaphore()
    for peer in everyone:
        pl.semaphore_signal(barrier, inc=1, device_id=peer, device_id_type=MESH)
    ways = ((planes, column_peer, z), (plane, plane_peer, m))
    own = [
        pltpu.make_async_copy(lat.at[c], gat[c].at[ways[c][2]], own_sem.at[c]) for c in range(2)
    ]
    tables = [
        pltpu.make_async_copy(owner_hbm, owner, own_sem.at[2]),
        pltpu.make_async_copy(counts_hbm, counts, own_sem.at[3]),
    ]
    for copy in own + tables:
        copy.start()

    def start_loads():
        for load in loads:
            load.start()

    def products():
        l_key.wait()
        l_query.wait()
        qk_t[...] = dot_nt(v_key[...], v_query[...]).astype(BF16)
        l_value.wait()
        l_out.wait()
        vo_t[0:ch, :] = dot(v_value[...], v_out[...]).T.astype(BF16)
        l_head.wait()
        wide = v_head[...].astype(F32)
        gap = jnp.zeros((1, ch), F32)
        head16[...] = jnp.concatenate(
            [wide[0:3], gap, wide[3:6], gap, wide[6:9], gap, wide[9:12], gap], axis=0
        ).astype(BF16)
        l_time.wait()
        for k in range(3):
            taps[16 * k : 16 * k + 16, :] = dot_nt(head16[...], v_time[2 - k]).astype(BF16)

        l_in.wait()
        in_t[0:ch, :] = v_in[...].astype(F32).T.astype(BF16)
        in_t[ch : ch + 16, :] = dot_nt(head16[...], v_in[...]).astype(BF16)
        vo_t[ch : ch + 16, :] = dot(head16[...], vo_t[0:ch, :]).astype(BF16)
        l_space.wait()

        def fold(i):
            got = dot_nt(taps[...], v_space[i]).astype(BF16)
            for k in range(3):
                eff[k, i] = got[16 * k : 16 * k + 16]

        for i in range(9):
            fold(i)

        r_id = lax.broadcasted_iota(jnp.int32, (PAIR, PAIR), 0)
        c_id = lax.broadcasted_iota(jnp.int32, (PAIR, PAIR), 1)
        goal = jnp.where(r_id < WIDE, 2 * r_id, 2 * (r_id - WIDE) + 1)
        spread_cols[...] = jnp.where(goal == c_id, 1.0, 0.0).astype(BF16)
        parts[...] = jnp.zeros(parts.shape, F32)

    early = z + lax.rem(m, 2) + m // 2 < planes // 2

    @pl.when(early)
    def _():
        start_loads()
        products()

    for copy in own:
        copy.wait()
    pl.semaphore_wait(barrier, len(everyone))

    gathers = ([], [])
    for c in range(2):
        count, peer, place = ways[c]
        for d in sorted(range(1, count), key=lambda d: -min(d, count - d)):
            copy = pltpu.make_async_remote_copy(
                src_ref=gat[c].at[place],
                dst_ref=gat[c].at[place],
                send_sem=g_send.at[c, d],
                recv_sem=g_recv.at[c, d],
                device_id=peer(d),
                device_id_type=MESH,
            )
            copy.start()
            gathers[c].append(copy)

    pl.when(jnp.logical_not(early))(start_loads)
    for copy in tables:
        copy.wait()

    picks = ([], [])
    for d in range(plane):
        slot = base + lax.rem(m + d, plane)
        pick = jnp.int32(0)
        for i in range(planes):
            pick = jnp.where(owner[i * plane + m] == slot, jnp.int32(i), pick)
        picks[0].append(pick)
    for d in range(planes):
        slot = lax.rem(z + d, planes) * plane + m
        pick = jnp.int32(0)
        for i in range(plane):
            pick = jnp.where(owner[base + i] == slot, jnp.int32(i), pick)
        picks[1].append(pick)

    passes = []
    for c in (1, 0):
        count, peer, _ = ways[1 - c]
        for copy in gathers[c]:
            copy.wait_recv()
        for d in sorted(range(count), key=lambda d: -min(d, count - d)):
            block = gat[c][picks[c][d]]
            if d == 0:
                got[c][0] = block
                continue
            p_buf[c, d] = block
            copy = pltpu.make_async_remote_copy(
                src_ref=p_buf.at[c, d],
                dst_ref=got[c].at[d],
                send_sem=p_send.at[c, d],
                recv_sem=p_recv.at[c, d],
                device_id=peer(d),
                device_id_type=MESH,
            )
            copy.start()
            passes.append(copy)

    def scan(g, carry):
        from_a, from_b, live = carry
        here = owner[g] == me
        step_a = lax.rem(m - lax.rem(g, plane) + plane, plane)
        step_b = lax.rem(z - g // plane + planes, planes)
        return (
            jnp.where(here, step_a, from_a),
            jnp.where(here, step_b, from_b),
            jnp.where(here, counts[g], live),
        )

    from_a, from_b, live = lax.fori_loop(0, plane * planes, scan, (jnp.int32(0),) * 3, unroll=8)

    pl.when(jnp.logical_not(early))(products)

    for copy in passes:
        copy.wait_recv()
    quarter[0] = got_a[from_a]
    quarter[1] = got_b[from_b]

    def exchange(i, src, dst, peer, sems):
        copy = pltpu.make_async_remote_copy(
            src_ref=src,
            dst_ref=dst,
            send_sem=sems[0].at[i],
            recv_sem=sems[1].at[i],
            device_id=peer,
            device_id_type=MESH,
        )
        copy.start()
        return copy

    frames = pl.ds(2 * t, 2)
    sems = (x_send, x_recv)
    rows = [
        exchange(0, quarter.at[:, pl.ds(1 - t, 3)], panel.at[frames, pl.ds(t, 3)], x_peers[0], sems),
        exchange(1, quarter.at[:, 3 * (1 - s)], panel.at[frames, 3 * t], x_peers[1], sems),
        exchange(2, quarter.at[:, 3 * (1 - s)], panel.at[frames, 3 * (1 - t)], x_peers[2], sems),
    ]
    for f in range(2):
        for r in range(3):
            panel[2 * t + f, 1 - t + r] = quarter[f, t + r]

    for copy in rows:
        copy.wait_recv()

    lane = lax.broadcasted_iota(jnp.int32, (16, WIDE), 1)
    top = jnp.logical_not(jnp.logical_and(s == 0, t == 0))
    bottom = jnp.logical_not(jnp.logical_and(s == 1, t == 1))
    for f in range(4):
        for r in range(4):
            tile = panel[f, r].astype(F32)
            if r == 0:
                tile = jnp.where(top, tile, 0.0)
            if r == 3:
                tile = jnp.where(bottom, tile, 0.0)
            left = jnp.where(lane == 0, 0.0, pltpu.roll(tile, 1, 1))
            right = jnp.where(lane == WIDE - 1, 0.0, pltpu.roll(tile, WIDE - 1, 1))
            for b, value in enumerate((left, tile, right)):
                value = value.astype(BF16)
                for a in range(3):
                    row = r - a
                    if row in (0, 1):
                        start = 16 * (3 * a + b)
                        patches[f, start : start + 16, row * WIDE : (row + 1) * WIDE] = value

    def inverse_rms(square):
        return lax.rsqrt(jnp.sum(square, axis=0, keepdims=True) / ch + EPS)

    tiles = [slice(c, c + 16) for c in range(0, ch, 16)]

    for f in range(4):
        wide = dot(in_t[...], patches[f])
        head_sum[f] = wide[ch : ch + 16]
        square = jnp.zeros((16, PAIR), F32)
        for c in tiles:
            x = wide[c]
            first[f, c, :] = x
            square = square + x * x
        scale = inverse_rms(square)
        for c in tiles:
            normal[f, c, :] = (first[f, c, :] * scale).astype(BF16)

    def make_query(f):
        query[f] = dot(qk_t[...], normal[f]).astype(BF16)

    def attend(f):
        accs = [jnp.zeros((16, PAIR), F32)] * (f + 1)
        for c in range(0, ch, 64):
            for g in range(f + 1):
                p = [
                    query[f, i : i + 16, :] * normal[g, i : i + 16, :]
                    for i in range(c, c + 64, 16)
                ]
                accs[g] = accs[g] + ((p[0] + p[1]) + (p[2] + p[3])).astype(F32)
        scores = [jnp.sum(acc, axis=0, keepdims=True) * (1.0 / math.sqrt(ch)) for acc in accs]
        highest = functools.reduce(jnp.maximum, scores)
        weights = [jnp.exp(x - highest) for x in scores]
        norm = 1.0 / functools.reduce(jnp.add, weights)
        weights = [jnp.broadcast_to(w * norm, (16, PAIR)).astype(BF16) for w in weights]
        for c in tiles:
            mixed[f, c, :] = functools.reduce(
                jnp.add, [w * normal[g, c, :] for g, w in enumerate(weights)]
            )

    def activate(f):
        wide = dot(vo_t[...], mixed[f])
        head = head_sum[f] + wide[ch : ch + 16]
        for row in range(2):
            spot = (f, row + 1)
            parts[spot] = parts[spot] + head[:, row * WIDE : (row + 1) * WIDE]
        square = jnp.zeros((16, PAIR), F32)
        for c in tiles:
            x = first[f, c, :] + wide[c]
            first[f, c, :] = x
            square = square + x * x
        scale = inverse_rms(square) * 0.5
        for c in tiles:
            x = first[f, c, :] * scale
            active[f, c, :] = (x + x * jnp.tanh(x)).astype(BF16)

    def spread(f):
        steps = min(3, 4 - f)
        wide = dot(eff[0:steps].reshape(144 * steps, ch), active[f])
        for k in range(steps):
            for r in range(4):
                sides = []
                for b in range(3):
                    pieces = []
                    for row in range(2):
                        a = row + 2 - r
                        if 0 <= a < 3:
                            start = 144 * k + 16 * (3 * a + b)
                            here = slice(row * WIDE, (row + 1) * WIDE)
                            pieces.append(wide[start : start + 16, here])
                    sides.append(functools.reduce(jnp.add, pieces))
                left = jnp.where(lane == 0, 0.0, pltpu.roll(sides[0], 1, 1))
                right = jnp.where(lane == WIDE - 1, 0.0, pltpu.roll(sides[2], WIDE - 1, 1))
                parts[f + k, r] = parts[f + k, r] + (sides[1] + (left + right))

    make_query(0)
    for f in range(4):
        if f < 3:
            make_query(f + 1)
        attend(f)
        activate(f)
        if f > 0:
            spread(f - 1)
    spread(3)

    for f in range(2):
        for r in range(3):
            to_tm[f, r] = parts[2 * (1 - t) + f, 1 - t + r].astype(BF16)
    for f in range(4):
        to_edge[f] = parts[f, 3 * t].astype(BF16)
    sems = (o_send, o_recv)
    coeffs = [
        exchange(0, to_tm, from_tm, x_peers[0], sems),
        exchange(1, to_edge.at[frames], from_edge.at[0], x_peers[1], sems),
        exchange(2, to_edge.at[pl.ds(2 * (1 - t), 2)], from_edge.at[1], x_peers[2], sems),
    ]
    owned[...] = jnp.zeros(owned.shape, F32)
    for f in range(2):
        for r in range(3):
            owned[f, t + r] = parts[2 * t + f, 1 - t + r]
    for copy in coeffs:
        copy.wait_recv()
    which = jnp.where(s == t, 0, 1)
    for f in range(2):
        for r in range(3):
            owned[f, 1 - t + r] = owned[f, 1 - t + r] + from_tm[f, r].astype(F32)
        edge = from_edge[which, f].astype(F32)
        owned[f, 3 * (1 - s)] = owned[f, 3 * (1 - s)] + edge

    for f in range(2):
        for h in range(4):
            low, high = owned[f, h, 0:8, :], owned[f, h, 8:16, :]
            for i, value in enumerate((low + high, low - high)):
                at = pl.ds(32 * f + 2 * h + i, 4, stride=8)
                pixel_rows[0, at, :] = (value[0:4] + value[4:8]) * 0.5
                pixel_rows[1, at, :] = (value[0:4] - value[4:8]) * 0.5
    both = jnp.concatenate([pixel_rows[0], pixel_rows[1]], axis=1)
    big = both.astype(BF16)
    small = (both - big.astype(F32)).astype(BF16)
    image = dot(big, spread_cols[...]) + dot(small, spread_cols[...])
    for f in range(2):
        keep = jnp.where(2 * t + f < live, 1.0, 0.0).astype(F32)
        for colour in range(3):
            start = 32 * f + 8 * colour
            out[0, f, colour] = image[start : start + 8] * keep

    for row in gathers:
        for copy in row:
            copy.wait_send()
    for copy in passes + rows + coeffs:
        copy.wait_send()


def solution(mesh):
    clips = mesh.shape["clip"]
    plane = 1 << (clips.bit_length() // 2)
    planes = clips // plane
    most = max(plane, planes)

    def body(
        gen_latent,
        frame_counts,
        owner_map,
        w_in,
        w_query,
        w_key,
        w_value,
        w_out,
        w_space,
        w_time,
        w_head,
    ):
        ch = w_query.shape[0]
        lat = jnp.swapaxes(gen_latent, -1, -2)[0]
        flat_in = w_in.reshape(144, ch)
        flat_space = w_space.reshape(9, ch, ch)
        vm = pltpu.VMEM
        dma = pltpu.SemaphoreType.DMA
        scratch = [
            vm((144, ch), BF16),
            vm((ch, ch), BF16),
            vm((ch, ch), BF16),
            vm((ch, ch), BF16),
            vm((ch, ch), BF16),
            vm((9, ch, ch), BF16),
            vm((3, ch, ch), BF16),
            vm((12, ch), BF16),
            pltpu.SMEM((clips,), jnp.int32),
            pltpu.SMEM((clips,), jnp.int32),
            vm((ch + 16, 144), BF16),
            vm((16, ch), BF16),
            vm((ch, ch), BF16),
            vm((ch + 16, ch), BF16),
            vm((48, ch), BF16),
            vm((3, 9, 16, ch), BF16),
            vm((PAIR, PAIR), BF16),
            vm((planes, 4, 16, WIDE), BF16),
            vm((plane, 4, 16, WIDE), BF16),
            vm((2, most, 4, 16, WIDE), BF16),
            vm((plane, 4, 16, WIDE), BF16),
            vm((planes, 4, 16, WIDE), BF16),
            vm((2, 4, 16, WIDE), BF16),
            vm((4, 4, 16, WIDE), BF16),
            vm((4, 144, PAIR), BF16),
            vm((4, ch, PAIR), F32),
            vm((4, ch, PAIR), BF16),
            vm((4, ch, PAIR), BF16),
            vm((4, ch, PAIR), BF16),
            vm((4, ch, PAIR), BF16),
            vm((4, 16, PAIR), F32),
            vm((4, 4, 16, WIDE), F32),
            vm((2, 3, 16, WIDE), BF16),
            vm((4, 16, WIDE), BF16),
            vm((2, 3, 16, WIDE), BF16),
            vm((2, 2, 16, WIDE), BF16),
            vm((2, 4, 16, WIDE), F32),
            vm((2, 64, WIDE), F32),
            dma((8,)),
            dma((4,)),
            dma((2, most)),
            dma((2, most)),
            dma((2, most)),
            dma((2, most)),
            dma((3,)),
            dma((3,)),
            dma((3,)),
            dma((3,)),
        ]
        hbm = pl.BlockSpec(memory_space=pltpu.HBM)
        return pl.pallas_call(
            functools.partial(kernel, plane, planes),
            out_shape=pltpu.VMEM((1, 2, 3, 8, 2 * WIDE), F32),
            in_specs=[hbm] * 11,
            out_specs=pl.BlockSpec(memory_space=pltpu.VMEM),
            scratch_shapes=scratch,
            compiler_params=pltpu.CompilerParams(
                collective_id=0, has_side_effects=True, vmem_limit_bytes=62 * 1024 * 1024
            ),
        )(
            owner_map,
            frame_counts,
            lat,
            flat_in,
            w_query,
            w_key,
            w_value,
            w_out,
            flat_space,
            w_time,
            w_head.T,
        )

    return jax.shard_map(
        body,
        mesh=mesh,
        in_specs=(P("clip", "tm", "space", None, None),) + (P(),) * 10,
        out_specs=P("clip", "tm", None, "space", None),
        check_vma=False,
    )
```

```python
import functools
import math

import jax
import jax.numpy as jnp
from jax import lax
from jax.experimental import pallas as pl
from jax.experimental.pallas import tpu as pltpu
from jax.sharding import PartitionSpec as P

EPS = 1e-06
MESH = pl.DeviceIdType.MESH
F32 = jnp.float32
BF16 = jnp.bfloat16
WIDE = 128
PAIR = 2 * WIDE


def dot(a, b):
    return jnp.dot(a, b, preferred_element_type=F32)


def dot_nt(a, b):
    return lax.dot_general(a, b, (((1,), (1,)), ((), ())), preferred_element_type=F32)


def kernel(
    plane,
    planes,
    owner_hbm,
    counts_hbm,
    lat,
    w_in,
    w_query,
    w_key,
    w_value,
    w_out,
    w_space,
    w_time,
    w_head,
    out,
    v_in,
    v_query,
    v_key,
    v_value,
    v_out,
    v_space,
    v_time,
    v_head,
    owner,
    counts,
    in_t,
    head16,
    qk_t,
    vo_t,
    taps,
    eff,
    spread_cols,
    gat_a,
    gat_b,
    p_buf,
    got_a,
    got_b,
    quarter,
    panel,
    patches,
    first,
    second,
    normal,
    query,
    mixed,
    active,
    parts,
    to_tm,
    to_edge,
    from_tm,
    from_edge,
    owned,
    pixel_rows,
    w_sem,
    own_sem,
    g_send,
    g_recv,
    p_send,
    p_recv,
    x_send,
    x_recv,
    o_send,
    o_recv,
):
    ch = v_query.shape[0]
    me = lax.axis_index("clip")
    s = lax.axis_index("space")
    t = lax.axis_index("tm")
    m = lax.rem(me, plane)
    z = me // plane
    base = z * plane
    gat = (gat_a, gat_b)
    got = (got_a, got_b)

    loads = [
        pltpu.make_async_copy(src, dst, w_sem.at[i])
        for i, (src, dst) in enumerate(
            (
                (w_key, v_key),
                (w_query, v_query),
                (w_value, v_value),
                (w_out, v_out),
                (w_head, v_head),
                (w_in, v_in),
                (w_time, v_time),
                (w_space, v_space),
            )
        )
    ]
    l_key, l_query, l_value, l_out, l_head, l_in, l_time, l_space = loads

    def plane_peer(d):
        return (base + lax.rem(m + d, plane), s, t)

    def column_peer(d):
        return (lax.rem(z + d, planes) * plane + m, s, t)

    x_peers = [(me, s, 1 - t), (me, 1 - s, t), (me, 1 - s, 1 - t)]
    everyone = [plane_peer(d) for d in range(1, plane)]
    everyone += [column_peer(d) for d in range(1, planes)] + x_peers
    barrier = pltpu.get_barrier_semaphore()
    for peer in everyone:
        pl.semaphore_signal(barrier, inc=1, device_id=peer, device_id_type=MESH)
    ways = ((planes, column_peer, z), (plane, plane_peer, m))
    own = [
        pltpu.make_async_copy(lat.at[c], gat[c].at[ways[c][2]], own_sem.at[c]) for c in range(2)
    ]
    tables = [
        pltpu.make_async_copy(owner_hbm, owner, own_sem.at[2]),
        pltpu.make_async_copy(counts_hbm, counts, own_sem.at[3]),
    ]
    for copy in own + tables:
        copy.start()

    def start_loads():
        for load in loads:
            load.start()

    def products():
        l_key.wait()
        l_query.wait()
        qk_t[...] = dot_nt(v_key[...], v_query[...]).astype(BF16)
        l_value.wait()
        l_out.wait()
        vo_t[0:ch, :] = dot(v_value[...], v_out[...]).T.astype(BF16)
        l_head.wait()
        wide = v_head[...].astype(F32)
        gap = jnp.zeros((1, ch), F32)
        head16[...] = jnp.concatenate(
            [wide[0:3], gap, wide[3:6], gap, wide[6:9], gap, wide[9:12], gap], axis=0
        ).astype(BF16)
        l_time.wait()
        for k in range(3):
            taps[16 * k : 16 * k + 16, :] = dot_nt(head16[...], v_time[2 - k]).astype(BF16)

        l_in.wait()
        in_t[0:ch, :] = v_in[...].astype(F32).T.astype(BF16)
        in_t[ch : ch + 16, :] = dot_nt(head16[...], v_in[...]).astype(BF16)
        vo_t[ch : ch + 16, :] = dot(head16[...], vo_t[0:ch, :]).astype(BF16)
        l_space.wait()

        def fold(i):
            got = dot_nt(taps[...], v_space[i]).astype(BF16)
            for k in range(3):
                eff[k, i] = got[16 * k : 16 * k + 16]

        for i in range(9):
            fold(i)

        r_id = lax.broadcasted_iota(jnp.int32, (PAIR, PAIR), 0)
        c_id = lax.broadcasted_iota(jnp.int32, (PAIR, PAIR), 1)
        goal = jnp.where(r_id < WIDE, 2 * r_id, 2 * (r_id - WIDE) + 1)
        spread_cols[...] = jnp.where(goal == c_id, 1.0, 0.0).astype(BF16)
        parts[...] = jnp.zeros(parts.shape, F32)

    early = z + lax.rem(m, 2) + m // 2 < planes // 2

    @pl.when(early)
    def _():
        start_loads()
        products()

    for copy in own:
        copy.wait()
    pl.semaphore_wait(barrier, len(everyone))

    gathers = ([], [])
    for c in range(2):
        count, peer, place = ways[c]
        for d in sorted(range(1, count), key=lambda d: -min(d, count - d)):
            copy = pltpu.make_async_remote_copy(
                src_ref=gat[c].at[place],
                dst_ref=gat[c].at[place],
                send_sem=g_send.at[c, d],
                recv_sem=g_recv.at[c, d],
                device_id=peer(d),
                device_id_type=MESH,
            )
            copy.start()
            gathers[c].append(copy)

    pl.when(jnp.logical_not(early))(start_loads)
    for copy in tables:
        copy.wait()

    picks = ([], [])
    for d in range(plane):
        slot = base + lax.rem(m + d, plane)
        pick = jnp.int32(0)
        for i in range(planes):
            pick = jnp.where(owner[i * plane + m] == slot, jnp.int32(i), pick)
        picks[0].append(pick)
    for d in range(planes):
        slot = lax.rem(z + d, planes) * plane + m
        pick = jnp.int32(0)
        for i in range(plane):
            pick = jnp.where(owner[base + i] == slot, jnp.int32(i), pick)
        picks[1].append(pick)

    passes = []
    for c in (1, 0):
        count, peer, _ = ways[1 - c]
        for copy in gathers[c]:
            copy.wait_recv()
        for d in sorted(range(count), key=lambda d: -min(d, count - d)):
            block = gat[c][picks[c][d]]
            if d == 0:
                got[c][0] = block
                continue
            p_buf[c, d] = block
            copy = pltpu.make_async_remote_copy(
                src_ref=p_buf.at[c, d],
                dst_ref=got[c].at[d],
                send_sem=p_send.at[c, d],
                recv_sem=p_recv.at[c, d],
                device_id=peer(d),
                device_id_type=MESH,
            )
            copy.start()
            passes.append(copy)

    def scan(g, carry):
        from_a, from_b, live = carry
        here = owner[g] == me
        step_a = lax.rem(m - lax.rem(g, plane) + plane, plane)
        step_b = lax.rem(z - g // plane + planes, planes)
        return (
            jnp.where(here, step_a, from_a),
            jnp.where(here, step_b, from_b),
            jnp.where(here, counts[g], live),
        )

    from_a, from_b, live = lax.fori_loop(0, plane * planes, scan, (jnp.int32(0),) * 3, unroll=8)

    pl.when(jnp.logical_not(early))(products)

    for copy in passes:
        copy.wait_recv()
    quarter[0] = got_a[from_a]
    quarter[1] = got_b[from_b]

    def exchange(i, src, dst, peer, sems):
        copy = pltpu.make_async_remote_copy(
            src_ref=src,
            dst_ref=dst,
            send_sem=sems[0].at[i],
            recv_sem=sems[1].at[i],
            device_id=peer,
            device_id_type=MESH,
        )
        copy.start()
        return copy

    frames = pl.ds(2 * t, 2)
    sems = (x_send, x_recv)
    rows = [
        exchange(0, quarter.at[:, pl.ds(1 - t, 3)], panel.at[frames, pl.ds(t, 3)], x_peers[0], sems),
        exchange(1, quarter.at[:, 3 * (1 - s)], panel.at[frames, 3 * t], x_peers[1], sems),
        exchange(2, quarter.at[:, 3 * (1 - s)], panel.at[frames, 3 * (1 - t)], x_peers[2], sems),
    ]
    for f in range(2):
        for r in range(3):
            panel[2 * t + f, 1 - t + r] = quarter[f, t + r]

    for copy in rows:
        copy.wait_recv()

    lane = lax.broadcasted_iota(jnp.int32, (16, WIDE), 1)
    top = jnp.logical_not(jnp.logical_and(s == 0, t == 0))
    bottom = jnp.logical_not(jnp.logical_and(s == 1, t == 1))
    for f in range(4):
        for r in range(4):
            tile = panel[f, r].astype(F32)
            if r == 0:
                tile = jnp.where(top, tile, 0.0)
            if r == 3:
                tile = jnp.where(bottom, tile, 0.0)
            left = jnp.where(lane == 0, 0.0, pltpu.roll(tile, 1, 1))
            right = jnp.where(lane == WIDE - 1, 0.0, pltpu.roll(tile, WIDE - 1, 1))
            for b, value in enumerate((left, tile, right)):
                value = value.astype(BF16)
                for a in range(3):
                    row = r - a
                    if row in (0, 1):
                        start = 16 * (3 * a + b)
                        patches[f, start : start + 16, row * WIDE : (row + 1) * WIDE] = value

    def inverse_rms(square):
        return lax.rsqrt(jnp.sum(square, axis=0, keepdims=True) / ch + EPS)

    tiles = [slice(c, c + 16) for c in range(0, ch, 16)]

    for f in range(4):
        first[f] = dot(in_t[...], patches[f])

    def make_query(f):
        square = jnp.zeros((16, PAIR), F32)
        for c in tiles:
            x = first[f, c, :]
            square = square + x * x
        scale = inverse_rms(square)
        for c in tiles:
            normal[f, c, :] = (first[f, c, :] * scale).astype(BF16)
        query[f] = dot(qk_t[...], normal[f]).astype(BF16)

    def attend(f):
        accs = [jnp.zeros((16, PAIR), F32)] * (f + 1)
        for c in range(0, ch, 64):
            for g in range(f + 1):
                p = [
                    query[f, i : i + 16, :] * normal[g, i : i + 16, :]
                    for i in range(c, c + 64, 16)
                ]
                accs[g] = accs[g] + ((p[0] + p[1]) + (p[2] + p[3])).astype(F32)
        scores = [jnp.sum(acc, axis=0, keepdims=True) * (1.0 / math.sqrt(ch)) for acc in accs]
        highest = functools.reduce(jnp.maximum, scores)
        weights = [jnp.exp(x - highest) for x in scores]
        norm = 1.0 / functools.reduce(jnp.add, weights)
        weights = [jnp.broadcast_to(w * norm, (16, PAIR)).astype(BF16) for w in weights]
        for c in tiles:
            mixed[f, c, :] = functools.reduce(
                jnp.add, [w * normal[g, c, :] for g, w in enumerate(weights)]
            )

    def project(f):
        second[f] = dot(vo_t[...], mixed[f])

    def activate(f):
        square = jnp.zeros((16, PAIR), F32)
        for c in tiles:
            x = first[f, c, :] + second[f, c, :]
            second[f, c, :] = x
            square = square + x * x
        scale = inverse_rms(square) * 0.5
        for c in tiles:
            x = second[f, c, :] * scale
            active[f, c, :] = (x + x * jnp.tanh(x)).astype(BF16)
        for row in range(2):
            here = slice(row * WIDE, (row + 1) * WIDE)
            head = first[f, ch : ch + 16, here] + second[f, ch : ch + 16, here]
            parts[f, row + 1] = parts[f, row + 1] + head

    def spread(f):
        steps = min(3, 4 - f)
        wide = dot(eff[0:steps].reshape(144 * steps, ch), active[f])
        for k in range(steps):
            for r in range(4):
                sides = []
                for b in range(3):
                    pieces = []
                    for row in range(2):
                        a = row + 2 - r
                        if 0 <= a < 3:
                            start = 144 * k + 16 * (3 * a + b)
                            here = slice(row * WIDE, (row + 1) * WIDE)
                            pieces.append(wide[start : start + 16, here])
                    sides.append(functools.reduce(jnp.add, pieces))
                left = jnp.where(lane == 0, 0.0, pltpu.roll(sides[0], 1, 1))
                right = jnp.where(lane == WIDE - 1, 0.0, pltpu.roll(sides[2], WIDE - 1, 1))
                parts[f + k, r] = parts[f + k, r] + (sides[1] + (left + right))

    for f in range(4):
        make_query(f)
    attend(0)
    project(0)
    attend(1)
    project(1)
    activate(0)
    attend(2)
    project(2)
    spread(0)
    activate(1)
    attend(3)
    project(3)
    spread(1)
    activate(2)
    spread(2)
    activate(3)
    spread(3)

    for f in range(2):
        for r in range(3):
            to_tm[f, r] = parts[2 * (1 - t) + f, 1 - t + r].astype(BF16)
    for f in range(4):
        to_edge[f] = parts[f, 3 * t].astype(BF16)
    sems = (o_send, o_recv)
    coeffs = [
        exchange(0, to_tm, from_tm, x_peers[0], sems),
        exchange(1, to_edge.at[frames], from_edge.at[0], x_peers[1], sems),
        exchange(2, to_edge.at[pl.ds(2 * (1 - t), 2)], from_edge.at[1], x_peers[2], sems),
    ]
    owned[...] = jnp.zeros(owned.shape, F32)
    for f in range(2):
        for r in range(3):
            owned[f, t + r] = parts[2 * t + f, 1 - t + r]
    for copy in coeffs:
        copy.wait_recv()
    which = jnp.where(s == t, 0, 1)
    for f in range(2):
        for r in range(3):
            owned[f, 1 - t + r] = owned[f, 1 - t + r] + from_tm[f, r].astype(F32)
        edge = from_edge[which, f].astype(F32)
        owned[f, 3 * (1 - s)] = owned[f, 3 * (1 - s)] + edge

    for f in range(2):
        for h in range(4):
            low, high = owned[f, h, 0:8, :], owned[f, h, 8:16, :]
            for i, value in enumerate((low + high, low - high)):
                at = pl.ds(32 * f + 2 * h + i, 4, stride=8)
                pixel_rows[0, at, :] = (value[0:4] + value[4:8]) * 0.5
                pixel_rows[1, at, :] = (value[0:4] - value[4:8]) * 0.5
    both = jnp.concatenate([pixel_rows[0], pixel_rows[1]], axis=1)
    big = both.astype(BF16)
    small = (both - big.astype(F32)).astype(BF16)
    image = dot(big, spread_cols[...]) + dot(small, spread_cols[...])
    for f in range(2):
        keep = jnp.where(2 * t + f < live, 1.0, 0.0).astype(F32)
        for colour in range(3):
            start = 32 * f + 8 * colour
            out[0, f, colour] = image[start : start + 8] * keep

    for row in gathers:
        for copy in row:
            copy.wait_send()
    for copy in passes + rows + coeffs:
        copy.wait_send()


def solution(mesh):
    clips = mesh.shape["clip"]
    plane = 1 << (clips.bit_length() // 2)
    planes = clips // plane
    most = max(plane, planes)

    def body(
        gen_latent,
        frame_counts,
        owner_map,
        w_in,
        w_query,
        w_key,
        w_value,
        w_out,
        w_space,
        w_time,
        w_head,
    ):
        ch = w_query.shape[0]
        lat = jnp.swapaxes(gen_latent, -1, -2)[0]
        flat_in = w_in.reshape(144, ch)
        flat_space = w_space.reshape(9, ch, ch)
        vm = pltpu.VMEM
        dma = pltpu.SemaphoreType.DMA
        scratch = [
            vm((144, ch), BF16),
            vm((ch, ch), BF16),
            vm((ch, ch), BF16),
            vm((ch, ch), BF16),
            vm((ch, ch), BF16),
            vm((9, ch, ch), BF16),
            vm((3, ch, ch), BF16),
            vm((12, ch), BF16),
            pltpu.SMEM((clips,), jnp.int32),
            pltpu.SMEM((clips,), jnp.int32),
            vm((ch + 16, 144), BF16),
            vm((16, ch), BF16),
            vm((ch, ch), BF16),
            vm((ch + 16, ch), BF16),
            vm((48, ch), BF16),
            vm((3, 9, 16, ch), BF16),
            vm((PAIR, PAIR), BF16),
            vm((planes, 4, 16, WIDE), BF16),
            vm((plane, 4, 16, WIDE), BF16),
            vm((2, most, 4, 16, WIDE), BF16),
            vm((plane, 4, 16, WIDE), BF16),
            vm((planes, 4, 16, WIDE), BF16),
            vm((2, 4, 16, WIDE), BF16),
            vm((4, 4, 16, WIDE), BF16),
            vm((4, 144, PAIR), BF16),
            vm((4, ch + 16, PAIR), F32),
            vm((4, ch + 16, PAIR), F32),
            vm((4, ch, PAIR), BF16),
            vm((4, ch, PAIR), BF16),
            vm((4, ch, PAIR), BF16),
            vm((4, ch, PAIR), BF16),
            vm((4, 4, 16, WIDE), F32),
            vm((2, 3, 16, WIDE), BF16),
            vm((4, 16, WIDE), BF16),
            vm((2, 3, 16, WIDE), BF16),
            vm((2, 2, 16, WIDE), BF16),
            vm((2, 4, 16, WIDE), F32),
            vm((2, 64, WIDE), F32),
            dma((8,)),
            dma((4,)),
            dma((2, most)),
            dma((2, most)),
            dma((2, most)),
            dma((2, most)),
            dma((3,)),
            dma((3,)),
            dma((3,)),
            dma((3,)),
        ]
        hbm = pl.BlockSpec(memory_space=pltpu.HBM)
        return pl.pallas_call(
            functools.partial(kernel, plane, planes),
            out_shape=pltpu.VMEM((1, 2, 3, 8, 2 * WIDE), F32),
            in_specs=[hbm] * 11,
            out_specs=pl.BlockSpec(memory_space=pltpu.VMEM),
            scratch_shapes=scratch,
            compiler_params=pltpu.CompilerParams(
                collective_id=0, has_side_effects=True, vmem_limit_bytes=62 * 1024 * 1024
            ),
        )(
            owner_map,
            frame_counts,
            lat,
            flat_in,
            w_query,
            w_key,
            w_value,
            w_out,
            flat_space,
            w_time,
            w_head.T,
        )

    return jax.shard_map(
        body,
        mesh=mesh,
        in_specs=(P("clip", "tm", "space", None, None),) + (P(),) * 10,
        out_specs=P("clip", "tm", None, "space", None),
        check_vma=False,
    )
```

```python
import functools
import math

import jax
import jax.numpy as jnp
from jax import lax
from jax.experimental import pallas as pl
from jax.experimental.pallas import tpu as pltpu
from jax.sharding import PartitionSpec as P

EPS = 1e-06
MESH = pl.DeviceIdType.MESH
F32 = jnp.float32
BF16 = jnp.bfloat16
WIDE = 128
PAIR = 2 * WIDE


def dot(a, b):
    return jnp.dot(a, b, preferred_element_type=F32)


def dot_nt(a, b):
    return lax.dot_general(a, b, (((1,), (1,)), ((), ())), preferred_element_type=F32)


def kernel(
    plane,
    planes,
    owner_hbm,
    counts_hbm,
    lat,
    w_in,
    w_query,
    w_key,
    w_value,
    w_out,
    w_space,
    w_time,
    w_head,
    out,
    v_in,
    v_query,
    v_key,
    v_value,
    v_out,
    v_space,
    v_time,
    v_head,
    owner,
    counts,
    in_t,
    head16,
    qk_t,
    vo_t,
    taps,
    eff,
    spread_cols,
    gat_a,
    gat_b,
    p_buf,
    got_a,
    got_b,
    quarter,
    panel,
    patches,
    first,
    second,
    normal,
    query,
    mixed,
    active,
    parts,
    to_tm,
    to_edge,
    from_tm,
    from_edge,
    owned,
    pixel_rows,
    w_sem,
    own_sem,
    g_send,
    g_recv,
    p_send,
    p_recv,
    x_send,
    x_recv,
    o_send,
    o_recv,
):
    ch = v_query.shape[0]
    me = lax.axis_index("clip")
    s = lax.axis_index("space")
    t = lax.axis_index("tm")
    m = lax.rem(me, plane)
    z = me // plane
    base = z * plane
    gat = (gat_a, gat_b)
    got = (got_a, got_b)

    loads = [
        pltpu.make_async_copy(src, dst, w_sem.at[i])
        for i, (src, dst) in enumerate(
            (
                (w_key, v_key),
                (w_query, v_query),
                (w_value, v_value),
                (w_out, v_out),
                (w_head, v_head),
                (w_in, v_in),
                (w_time, v_time),
                (w_space, v_space),
            )
        )
    ]
    l_key, l_query, l_value, l_out, l_head, l_in, l_time, l_space = loads

    def others(count, place):
        return [i + (i + count - place) // count for i in range(count - 1)]

    def plane_peer(q):
        return (base + q, s, t)

    def column_peer(q):
        return (q * plane + m, s, t)

    x_peers = [(me, s, 1 - t), (me, 1 - s, t), (me, 1 - s, 1 - t)]
    everyone = [plane_peer(q) for q in others(plane, m)]
    everyone += [column_peer(q) for q in others(planes, z)] + x_peers
    barrier = pltpu.get_barrier_semaphore()
    for peer in everyone:
        pl.semaphore_signal(barrier, inc=1, device_id=peer, device_id_type=MESH)
    ways = ((planes, column_peer, z), (plane, plane_peer, m))
    own = [
        pltpu.make_async_copy(lat.at[c], gat[c].at[ways[c][2]], own_sem.at[c]) for c in range(2)
    ]
    tables = [
        pltpu.make_async_copy(owner_hbm, owner, own_sem.at[2]),
        pltpu.make_async_copy(counts_hbm, counts, own_sem.at[3]),
    ]
    for copy in own + tables:
        copy.start()

    def start_loads():
        for load in loads:
            load.start()

    def products():
        l_key.wait()
        l_query.wait()
        qk_t[...] = dot_nt(v_key[...], v_query[...]).astype(BF16)
        l_value.wait()
        l_out.wait()
        vo_t[0:ch, :] = dot(v_value[...], v_out[...]).T.astype(BF16)
        l_head.wait()
        wide = v_head[...].astype(F32)
        gap = jnp.zeros((1, ch), F32)
        head16[...] = jnp.concatenate(
            [wide[0:3], gap, wide[3:6], gap, wide[6:9], gap, wide[9:12], gap], axis=0
        ).astype(BF16)
        l_time.wait()
        for k in range(3):
            taps[16 * k : 16 * k + 16, :] = dot_nt(head16[...], v_time[2 - k]).astype(BF16)

        l_in.wait()
        in_t[0:ch, :] = v_in[...].astype(F32).T.astype(BF16)
        in_t[ch : ch + 16, :] = dot_nt(head16[...], v_in[...]).astype(BF16)
        vo_t[ch : ch + 16, :] = dot(head16[...], vo_t[0:ch, :]).astype(BF16)
        l_space.wait()

        def fold(i):
            got = dot_nt(taps[...], v_space[i]).astype(BF16)
            for k in range(3):
                eff[k, i] = got[16 * k : 16 * k + 16]

        for i in range(9):
            fold(i)

        r_id = lax.broadcasted_iota(jnp.int32, (PAIR, PAIR), 0)
        c_id = lax.broadcasted_iota(jnp.int32, (PAIR, PAIR), 1)
        goal = jnp.where(r_id < WIDE, 2 * r_id, 2 * (r_id - WIDE) + 1)
        spread_cols[...] = jnp.where(goal == c_id, 1.0, 0.0).astype(BF16)
        parts[...] = jnp.zeros(parts.shape, F32)

    early = z + lax.rem(m, 2) + m // 2 < planes // 2

    last = jnp.logical_and(z >= planes // 2, m >= plane // 2)
    pl.when(jnp.logical_not(last))(start_loads)
    pl.when(early)(products)

    for copy in own:
        copy.wait()
    pl.semaphore_wait(barrier, len(everyone))

    def send(i, src, dst, sems, place, device):
        copy = pltpu.make_async_remote_copy(
            src_ref=src,
            dst_ref=dst,
            send_sem=sems[0].at[i],
            recv_sem=sems[1].at[place],
            device_id=device,
            device_id_type=MESH,
        )
        copy.start()
        return copy

    def arrive(dst, sems, place, device):
        pltpu.make_async_remote_copy(
            src_ref=dst,
            dst_ref=dst,
            send_sem=sems[0].at[0],
            recv_sem=sems[1].at[place],
            device_id=device,
            device_id_type=MESH,
        ).wait_recv()

    sent = []
    for c in range(2):
        count, peer, place = ways[c]
        sems = (g_send.at[c], g_recv.at[c])
        block = gat[c].at[place]
        for i, q in enumerate(others(count, place)):
            sent.append(send(i, block, block, sems, place, peer(q)))

    for copy in tables:
        copy.wait()

    def pick(c, q):
        found = jnp.int32(0)
        for i in range(ways[c][0]):
            here, goal = (i * plane + m, base + q) if c == 0 else (base + i, q * plane + m)
            found = jnp.where(owner[here] == goal, jnp.int32(i), found)
        return found

    for c in (1, 0):
        count, peer, place = ways[c]
        sems = (g_send.at[c], g_recv.at[c])
        for q in others(count, place):
            arrive(gat[c].at[q], sems, q, peer(q))
        count, peer, place = ways[1 - c]
        sems = (p_send.at[c], p_recv.at[c])
        for i, q in enumerate(others(count, place)):
            p_buf[c, i] = gat[c][pick(c, q)]
            sent.append(send(i, p_buf.at[c, i], got[c].at[place], sems, place, peer(q)))
        got[c][place] = gat[c][pick(c, place)]

    pl.when(last)(start_loads)

    def scan(g, carry):
        from_a, from_b, live = carry
        here = owner[g] == me
        return (
            jnp.where(here, lax.rem(g, plane), from_a),
            jnp.where(here, g // plane, from_b),
            jnp.where(here, counts[g], live),
        )

    from_a, from_b, live = lax.fori_loop(0, plane * planes, scan, (jnp.int32(0),) * 3, unroll=8)

    pl.when(jnp.logical_not(early))(products)

    for c in range(2):
        count, peer, place = ways[1 - c]
        for q in others(count, place):
            arrive(got[c].at[q], (p_send.at[c], p_recv.at[c]), q, peer(q))
    quarter[0] = got_a[from_a]
    quarter[1] = got_b[from_b]

    def exchange(i, src, dst, peer, sems):
        copy = pltpu.make_async_remote_copy(
            src_ref=src,
            dst_ref=dst,
            send_sem=sems[0].at[i],
            recv_sem=sems[1].at[i],
            device_id=peer,
            device_id_type=MESH,
        )
        copy.start()
        return copy

    frames = pl.ds(2 * t, 2)
    sems = (x_send, x_recv)
    rows = [
        exchange(0, quarter.at[:, pl.ds(1 - t, 3)], panel.at[frames, pl.ds(t, 3)], x_peers[0], sems),
        exchange(1, quarter.at[:, 3 * (1 - s)], panel.at[frames, 3 * t], x_peers[1], sems),
        exchange(2, quarter.at[:, 3 * (1 - s)], panel.at[frames, 3 * (1 - t)], x_peers[2], sems),
    ]
    for f in range(2):
        for r in range(3):
            panel[2 * t + f, 1 - t + r] = quarter[f, t + r]

    for copy in rows:
        copy.wait_recv()

    lane = lax.broadcasted_iota(jnp.int32, (16, WIDE), 1)
    top = jnp.logical_not(jnp.logical_and(s == 0, t == 0))
    bottom = jnp.logical_not(jnp.logical_and(s == 1, t == 1))
    for f in range(4):
        for r in range(4):
            tile = panel[f, r].astype(F32)
            if r == 0:
                tile = jnp.where(top, tile, 0.0)
            if r == 3:
                tile = jnp.where(bottom, tile, 0.0)
            left = jnp.where(lane == 0, 0.0, pltpu.roll(tile, 1, 1))
            right = jnp.where(lane == WIDE - 1, 0.0, pltpu.roll(tile, WIDE - 1, 1))
            for b, value in enumerate((left, tile, right)):
                value = value.astype(BF16)
                for a in range(3):
                    row = r - a
                    if row in (0, 1):
                        start = 16 * (3 * a + b)
                        patches[f, start : start + 16, row * WIDE : (row + 1) * WIDE] = value

    def inverse_rms(square):
        return lax.rsqrt(jnp.sum(square, axis=0, keepdims=True) / ch + EPS)

    tiles = [slice(c, c + 16) for c in range(0, ch, 16)]

    for f in range(4):
        first[f] = dot(in_t[...], patches[f])

    def make_query(f):
        square = jnp.zeros((16, PAIR), F32)
        for c in tiles:
            x = first[f, c, :]
            square = square + x * x
        scale = inverse_rms(square)
        for c in tiles:
            normal[f, c, :] = (first[f, c, :] * scale).astype(BF16)
        query[f] = dot(qk_t[...], normal[f]).astype(BF16)

    def attend(f):
        accs = [jnp.zeros((16, PAIR), F32)] * (f + 1)
        for c in range(0, ch, 64):
            for g in range(f + 1):
                p = [
                    query[f, i : i + 16, :] * normal[g, i : i + 16, :]
                    for i in range(c, c + 64, 16)
                ]
                accs[g] = accs[g] + ((p[0] + p[1]) + (p[2] + p[3])).astype(F32)
        scores = [jnp.sum(acc, axis=0, keepdims=True) * (1.0 / math.sqrt(ch)) for acc in accs]
        highest = functools.reduce(jnp.maximum, scores)
        weights = [jnp.exp(x - highest) for x in scores]
        norm = 1.0 / functools.reduce(jnp.add, weights)
        weights = [jnp.broadcast_to(w * norm, (16, PAIR)).astype(BF16) for w in weights]
        for c in tiles:
            mixed[f, c, :] = functools.reduce(
                jnp.add, [w * normal[g, c, :] for g, w in enumerate(weights)]
            )

    def project(f):
        second[f] = dot(vo_t[...], mixed[f])

    def activate(f):
        square = jnp.zeros((16, PAIR), F32)
        for c in tiles:
            x = first[f, c, :] + second[f, c, :]
            second[f, c, :] = x
            square = square + x * x
        scale = inverse_rms(square) * 0.5
        for c in tiles:
            x = second[f, c, :] * scale
            active[f, c, :] = (x + x * jnp.tanh(x)).astype(BF16)
        for row in range(2):
            here = slice(row * WIDE, (row + 1) * WIDE)
            head = first[f, ch : ch + 16, here] + second[f, ch : ch + 16, here]
            parts[f, row + 1] = parts[f, row + 1] + head

    def spread(f):
        steps = min(3, 4 - f)
        wide = dot(eff[0:steps].reshape(144 * steps, ch), active[f])
        for k in range(steps):
            for r in range(4):
                sides = []
                for b in range(3):
                    pieces = []
                    for row in range(2):
                        a = row + 2 - r
                        if 0 <= a < 3:
                            start = 144 * k + 16 * (3 * a + b)
                            here = slice(row * WIDE, (row + 1) * WIDE)
                            pieces.append(wide[start : start + 16, here])
                    sides.append(functools.reduce(jnp.add, pieces))
                left = jnp.where(lane == 0, 0.0, pltpu.roll(sides[0], 1, 1))
                right = jnp.where(lane == WIDE - 1, 0.0, pltpu.roll(sides[2], WIDE - 1, 1))
                parts[f + k, r] = parts[f + k, r] + (sides[1] + (left + right))

    for f in range(4):
        make_query(f)
    attend(0)
    project(0)
    attend(1)
    project(1)
    activate(0)
    attend(2)
    project(2)
    spread(0)
    activate(1)
    attend(3)
    project(3)
    spread(1)
    activate(2)
    spread(2)
    activate(3)
    spread(3)

    for f in range(2):
        for r in range(3):
            to_tm[f, r] = parts[2 * (1 - t) + f, 1 - t + r].astype(BF16)
    for f in range(4):
        to_edge[f] = parts[f, 3 * t].astype(BF16)
    sems = (o_send, o_recv)
    coeffs = [
        exchange(0, to_tm, from_tm, x_peers[0], sems),
        exchange(1, to_edge.at[frames], from_edge.at[0], x_peers[1], sems),
        exchange(2, to_edge.at[pl.ds(2 * (1 - t), 2)], from_edge.at[1], x_peers[2], sems),
    ]
    owned[...] = jnp.zeros(owned.shape, F32)
    for f in range(2):
        for r in range(3):
            owned[f, t + r] = parts[2 * t + f, 1 - t + r]
    for copy in coeffs:
        copy.wait_recv()
    which = jnp.where(s == t, 0, 1)
    for f in range(2):
        for r in range(3):
            owned[f, 1 - t + r] = owned[f, 1 - t + r] + from_tm[f, r].astype(F32)
        edge = from_edge[which, f].astype(F32)
        owned[f, 3 * (1 - s)] = owned[f, 3 * (1 - s)] + edge

    for f in range(2):
        for h in range(4):
            low, high = owned[f, h, 0:8, :], owned[f, h, 8:16, :]
            for i, value in enumerate((low + high, low - high)):
                at = pl.ds(32 * f + 2 * h + i, 4, stride=8)
                pixel_rows[0, at, :] = (value[0:4] + value[4:8]) * 0.5
                pixel_rows[1, at, :] = (value[0:4] - value[4:8]) * 0.5
    both = jnp.concatenate([pixel_rows[0], pixel_rows[1]], axis=1)
    big = both.astype(BF16)
    small = (both - big.astype(F32)).astype(BF16)
    image = dot(big, spread_cols[...]) + dot(small, spread_cols[...])
    for f in range(2):
        keep = jnp.where(2 * t + f < live, 1.0, 0.0).astype(F32)
        for colour in range(3):
            start = 32 * f + 8 * colour
            out[0, f, colour] = image[start : start + 8] * keep

    for copy in sent + rows + coeffs:
        copy.wait_send()


def solution(mesh):
    clips = mesh.shape["clip"]
    plane = 1 << (clips.bit_length() // 2)
    planes = clips // plane
    most = max(plane, planes)

    def body(
        gen_latent,
        frame_counts,
        owner_map,
        w_in,
        w_query,
        w_key,
        w_value,
        w_out,
        w_space,
        w_time,
        w_head,
    ):
        ch = w_query.shape[0]
        lat = jnp.swapaxes(gen_latent, -1, -2)[0]
        flat_in = w_in.reshape(144, ch)
        flat_space = w_space.reshape(9, ch, ch)
        vm = pltpu.VMEM
        dma = pltpu.SemaphoreType.DMA
        scratch = [
            vm((144, ch), BF16),
            vm((ch, ch), BF16),
            vm((ch, ch), BF16),
            vm((ch, ch), BF16),
            vm((ch, ch), BF16),
            vm((9, ch, ch), BF16),
            vm((3, ch, ch), BF16),
            vm((12, ch), BF16),
            pltpu.SMEM((clips,), jnp.int32),
            pltpu.SMEM((clips,), jnp.int32),
            vm((ch + 16, 144), BF16),
            vm((16, ch), BF16),
            vm((ch, ch), BF16),
            vm((ch + 16, ch), BF16),
            vm((48, ch), BF16),
            vm((3, 9, 16, ch), BF16),
            vm((PAIR, PAIR), BF16),
            vm((planes, 4, 16, WIDE), BF16),
            vm((plane, 4, 16, WIDE), BF16),
            vm((2, most, 4, 16, WIDE), BF16),
            vm((plane, 4, 16, WIDE), BF16),
            vm((planes, 4, 16, WIDE), BF16),
            vm((2, 4, 16, WIDE), BF16),
            vm((4, 4, 16, WIDE), BF16),
            vm((4, 144, PAIR), BF16),
            vm((4, ch + 16, PAIR), F32),
            vm((4, ch + 16, PAIR), F32),
            vm((4, ch, PAIR), BF16),
            vm((4, ch, PAIR), BF16),
            vm((4, ch, PAIR), BF16),
            vm((4, ch, PAIR), BF16),
            vm((4, 4, 16, WIDE), F32),
            vm((2, 3, 16, WIDE), BF16),
            vm((4, 16, WIDE), BF16),
            vm((2, 3, 16, WIDE), BF16),
            vm((2, 2, 16, WIDE), BF16),
            vm((2, 4, 16, WIDE), F32),
            vm((2, 64, WIDE), F32),
            dma((8,)),
            dma((4,)),
            dma((2, most)),
            dma((2, most)),
            dma((2, most)),
            dma((2, most)),
            dma((3,)),
            dma((3,)),
            dma((3,)),
            dma((3,)),
        ]
        hbm = pl.BlockSpec(memory_space=pltpu.HBM)
        return pl.pallas_call(
            functools.partial(kernel, plane, planes),
            out_shape=pltpu.VMEM((1, 2, 3, 8, 2 * WIDE), F32),
            in_specs=[hbm] * 11,
            out_specs=pl.BlockSpec(memory_space=pltpu.VMEM),
            scratch_shapes=scratch,
            compiler_params=pltpu.CompilerParams(
                collective_id=0, has_side_effects=True, vmem_limit_bytes=62 * 1024 * 1024
            ),
        )(
            owner_map,
            frame_counts,
            lat,
            flat_in,
            w_query,
            w_key,
            w_value,
            w_out,
            flat_space,
            w_time,
            w_head.T,
        )

    return jax.shard_map(
        body,
        mesh=mesh,
        in_specs=(P("clip", "tm", "space", None, None),) + (P(),) * 10,
        out_specs=P("clip", "tm", None, "space", None),
        check_vma=False,
    )
```

```python
import functools
import math

import jax
import jax.numpy as jnp
from jax import lax
from jax.experimental import pallas as pl
from jax.experimental.pallas import tpu as pltpu
from jax.sharding import PartitionSpec as P

EPS = 1e-06
MESH = pl.DeviceIdType.MESH
F32 = jnp.float32
BF16 = jnp.bfloat16
WIDE = 128
PAIR = 2 * WIDE


def dot(a, b):
    return jnp.dot(a, b, preferred_element_type=F32)


def dot_nt(a, b):
    return lax.dot_general(a, b, (((1,), (1,)), ((), ())), preferred_element_type=F32)


def kernel(
    plane,
    planes,
    owner_hbm,
    counts_hbm,
    lat,
    w_in,
    w_query,
    w_key,
    w_value,
    w_out,
    w_space,
    w_time,
    w_head,
    out,
    v_in,
    v_query,
    v_key,
    v_value,
    v_out,
    v_space,
    v_time,
    v_head,
    owner,
    counts,
    in_t,
    head16,
    qk_t,
    vo_t,
    taps,
    eff,
    spread_cols,
    gat_a,
    gat_b,
    p_buf,
    got_a,
    got_b,
    quarter,
    panel,
    patches,
    first,
    second,
    normal,
    query,
    mixed,
    active,
    parts,
    to_tm,
    to_edge,
    from_tm,
    from_edge,
    owned,
    pixel_rows,
    w_sem,
    own_sem,
    g_send,
    g_recv,
    p_send,
    p_recv,
    x_send,
    x_recv,
    o_send,
    o_recv,
):
    ch = v_query.shape[0]
    me = lax.axis_index("clip")
    s = lax.axis_index("space")
    t = lax.axis_index("tm")
    m = lax.rem(me, plane)
    z = me // plane
    base = z * plane
    gat = (gat_a, gat_b)
    got = (got_a, got_b)

    loads = [
        pltpu.make_async_copy(src, dst, w_sem.at[i])
        for i, (src, dst) in enumerate(
            (
                (w_key, v_key),
                (w_query, v_query),
                (w_value, v_value),
                (w_out, v_out),
                (w_head, v_head),
                (w_in, v_in),
                (w_time, v_time),
                (w_space, v_space),
            )
        )
    ]
    l_key, l_query, l_value, l_out, l_head, l_in, l_time, l_space = loads

    def others(count, place):
        return [i + (i + count - place) // count for i in range(count - 1)]

    def plane_peer(q):
        return (base + q, s, t)

    def column_peer(q):
        return (q * plane + m, s, t)

    x_peers = [(me, s, 1 - t), (me, 1 - s, t), (me, 1 - s, 1 - t)]
    everyone = [column_peer(q) for q in others(planes, z)] + x_peers
    everyone += [plane_peer(q) for q in others(plane, m)]
    barrier = pltpu.get_barrier_semaphore()
    for peer in everyone:
        pl.semaphore_signal(barrier, inc=1, device_id=peer, device_id_type=MESH)
    ways = ((planes, column_peer, z), (plane, plane_peer, m))
    own = [
        pltpu.make_async_copy(lat.at[1 - c], gat[c].at[ways[c][2]], own_sem.at[c]) for c in range(2)
    ]
    tables = [
        pltpu.make_async_copy(owner_hbm, owner, own_sem.at[2]),
        pltpu.make_async_copy(counts_hbm, counts, own_sem.at[3]),
    ]
    for copy in own + tables:
        copy.start()

    def start_loads():
        for load in loads:
            load.start()

    def products():
        l_key.wait()
        l_query.wait()
        qk_t[...] = dot_nt(v_key[...], v_query[...]).astype(BF16)
        l_value.wait()
        l_out.wait()
        vo_t[0:ch, :] = dot(v_value[...], v_out[...]).T.astype(BF16)
        l_head.wait()
        wide = v_head[...].astype(F32)
        gap = jnp.zeros((1, ch), F32)
        head16[...] = jnp.concatenate(
            [wide[0:3], gap, wide[3:6], gap, wide[6:9], gap, wide[9:12], gap], axis=0
        ).astype(BF16)
        l_time.wait()
        for k in range(3):
            taps[16 * k : 16 * k + 16, :] = dot_nt(head16[...], v_time[2 - k]).astype(BF16)

        l_in.wait()
        in_t[0:ch, :] = v_in[...].astype(F32).T.astype(BF16)
        in_t[ch : ch + 16, :] = dot_nt(head16[...], v_in[...]).astype(BF16)
        vo_t[ch : ch + 16, :] = dot(head16[...], vo_t[0:ch, :]).astype(BF16)
        l_space.wait()

        def fold(i):
            got = dot_nt(taps[...], v_space[i]).astype(BF16)
            for k in range(3):
                eff[k, i] = got[16 * k : 16 * k + 16]

        for i in range(9):
            fold(i)

        r_id = lax.broadcasted_iota(jnp.int32, (PAIR, PAIR), 0)
        c_id = lax.broadcasted_iota(jnp.int32, (PAIR, PAIR), 1)
        goal = jnp.where(r_id < WIDE, 2 * r_id, 2 * (r_id - WIDE) + 1)
        spread_cols[...] = jnp.where(goal == c_id, 1.0, 0.0).astype(BF16)
        parts[...] = jnp.zeros(parts.shape, F32)

    early = z + lax.rem(m, 2) + m // 2 < planes // 2

    last = jnp.logical_and(z >= planes // 2, m >= plane // 2)
    pl.when(jnp.logical_not(last))(start_loads)
    pl.when(early)(products)

    for copy in own:
        copy.wait()
    pl.semaphore_wait(barrier, len(everyone))

    def send(i, src, dst, sems, place, device):
        copy = pltpu.make_async_remote_copy(
            src_ref=src,
            dst_ref=dst,
            send_sem=sems[0].at[i],
            recv_sem=sems[1].at[place],
            device_id=device,
            device_id_type=MESH,
        )
        copy.start()
        return copy

    def arrive(dst, sems, place, device):
        pltpu.make_async_remote_copy(
            src_ref=dst,
            dst_ref=dst,
            send_sem=sems[0].at[0],
            recv_sem=sems[1].at[place],
            device_id=device,
            device_id_type=MESH,
        ).wait_recv()

    sent = []
    for c in (1, 0):
        count, peer, place = ways[c]
        sems = (g_send.at[c], g_recv.at[c])
        block = gat[c].at[place]
        for i, q in enumerate(others(count, place)):
            sent.append(send(i, block, block, sems, place, peer(q)))

    for copy in tables:
        copy.wait()

    def pick(c, q):
        found = jnp.int32(0)
        for i in range(ways[c][0]):
            here, goal = (i * plane + m, base + q) if c == 0 else (base + i, q * plane + m)
            found = jnp.where(owner[here] == goal, jnp.int32(i), found)
        return found

    for c in (1, 0):
        count, peer, place = ways[c]
        sems = (g_send.at[c], g_recv.at[c])
        for q in others(count, place):
            arrive(gat[c].at[q], sems, q, peer(q))
        count, peer, place = ways[1 - c]
        sems = (p_send.at[c], p_recv.at[c])
        for i, q in enumerate(others(count, place)):
            p_buf[c, i] = gat[c][pick(c, q)]
            sent.append(send(i, p_buf.at[c, i], got[c].at[place], sems, place, peer(q)))
        got[c][place] = gat[c][pick(c, place)]

    pl.when(last)(start_loads)

    def scan(g, carry):
        from_a, from_b, live = carry
        here = owner[g] == me
        return (
            jnp.where(here, lax.rem(g, plane), from_a),
            jnp.where(here, g // plane, from_b),
            jnp.where(here, counts[g], live),
        )

    from_a, from_b, live = lax.fori_loop(0, plane * planes, scan, (jnp.int32(0),) * 3, unroll=8)

    pl.when(jnp.logical_not(early))(products)

    def exchange(i, src, dst, peer, sems):
        copy = pltpu.make_async_remote_copy(
            src_ref=src,
            dst_ref=dst,
            send_sem=sems[0].at[i],
            recv_sem=sems[1].at[i],
            device_id=peer,
            device_id_type=MESH,
        )
        copy.start()
        return copy

    frames = pl.ds(2 * t, 2)
    rows = []
    for c in (1, 0):
        count, peer, place = ways[1 - c]
        for q in others(count, place):
            arrive(got[c].at[q], (p_send.at[c], p_recv.at[c]), q, peer(q))
        quarter[c] = got[c][(from_a, from_b)[c]]
        sems = (x_send.at[1 - c], x_recv.at[1 - c])
        near, edge = quarter.at[c, pl.ds(1 - t, 3)], quarter.at[c, 3 * (1 - s)]
        f = 2 * t + 1 - c
        rows += [
            exchange(0, near, panel.at[f, pl.ds(t, 3)], x_peers[0], sems),
            exchange(1, edge, panel.at[f, 3 * t], x_peers[1], sems),
            exchange(2, edge, panel.at[f, 3 * (1 - t)], x_peers[2], sems),
        ]
        for r in range(3):
            panel[f, 1 - t + r] = quarter[c, t + r]

    lane = lax.broadcasted_iota(jnp.int32, (16, WIDE), 1)
    top = jnp.logical_not(jnp.logical_and(s == 0, t == 0))
    bottom = jnp.logical_not(jnp.logical_and(s == 1, t == 1))
    def make_patches(f):
        for r in range(4):
            tile = panel[f, r].astype(F32)
            if r == 0:
                tile = jnp.where(top, tile, 0.0)
            if r == 3:
                tile = jnp.where(bottom, tile, 0.0)
            left = jnp.where(lane == 0, 0.0, pltpu.roll(tile, 1, 1))
            right = jnp.where(lane == WIDE - 1, 0.0, pltpu.roll(tile, WIDE - 1, 1))
            for b, value in enumerate((left, tile, right)):
                value = value.astype(BF16)
                for a in range(3):
                    row = r - a
                    if row in (0, 1):
                        start = 16 * (3 * a + b)
                        patches[f, start : start + 16, row * WIDE : (row + 1) * WIDE] = value

    def inverse_rms(square):
        return lax.rsqrt(jnp.sum(square, axis=0, keepdims=True) / ch + EPS)

    tiles = [slice(c, c + 16) for c in range(0, ch, 16)]

    def make_query(f):
        square = jnp.zeros((16, PAIR), F32)
        for c in tiles:
            x = first[f, c, :]
            square = square + x * x
        scale = inverse_rms(square)
        for c in tiles:
            normal[f, c, :] = (first[f, c, :] * scale).astype(BF16)
        query[f] = dot(qk_t[...], normal[f]).astype(BF16)

    def attend(f):
        accs = [jnp.zeros((16, PAIR), F32)] * (f + 1)
        for c in range(0, ch, 64):
            for g in range(f + 1):
                p = [
                    query[f, i : i + 16, :] * normal[g, i : i + 16, :]
                    for i in range(c, c + 64, 16)
                ]
                accs[g] = accs[g] + ((p[0] + p[1]) + (p[2] + p[3])).astype(F32)
        scores = [jnp.sum(acc, axis=0, keepdims=True) * (1.0 / math.sqrt(ch)) for acc in accs]
        highest = functools.reduce(jnp.maximum, scores)
        weights = [jnp.exp(x - highest) for x in scores]
        norm = 1.0 / functools.reduce(jnp.add, weights)
        weights = [jnp.broadcast_to(w * norm, (16, PAIR)).astype(BF16) for w in weights]
        for c in tiles:
            mixed[f, c, :] = functools.reduce(
                jnp.add, [w * normal[g, c, :] for g, w in enumerate(weights)]
            )

    def project(f):
        second[f] = dot(vo_t[...], mixed[f])

    def activate(f):
        square = jnp.zeros((16, PAIR), F32)
        for c in tiles:
            x = first[f, c, :] + second[f, c, :]
            second[f, c, :] = x
            square = square + x * x
        scale = inverse_rms(square) * 0.5
        for c in tiles:
            x = second[f, c, :] * scale
            active[f, c, :] = (x + x * jnp.tanh(x)).astype(BF16)
        for row in range(2):
            here = slice(row * WIDE, (row + 1) * WIDE)
            head = first[f, ch : ch + 16, here] + second[f, ch : ch + 16, here]
            parts[f, row + 1] = parts[f, row + 1] + head

    def spread(f):
        steps = min(3, 4 - f)
        wide = dot(eff[0:steps].reshape(144 * steps, ch), active[f])
        for k in range(steps):
            for r in range(4):
                sides = []
                for b in range(3):
                    pieces = []
                    for row in range(2):
                        a = row + 2 - r
                        if 0 <= a < 3:
                            start = 144 * k + 16 * (3 * a + b)
                            here = slice(row * WIDE, (row + 1) * WIDE)
                            pieces.append(wide[start : start + 16, here])
                    sides.append(functools.reduce(jnp.add, pieces))
                left = jnp.where(lane == 0, 0.0, pltpu.roll(sides[0], 1, 1))
                right = jnp.where(lane == WIDE - 1, 0.0, pltpu.roll(sides[2], WIDE - 1, 1))
                parts[f + k, r] = parts[f + k, r] + (sides[1] + (left + right))

    def begin(c):
        for copy in rows[3 * c : 3 * c + 3]:
            copy.wait_recv()
        for f in (c, c + 2):
            make_patches(f)
        for f in (c, c + 2):
            first[f] = dot(in_t[...], patches[f])
        for f in (c, c + 2):
            make_query(f)

    begin(0)
    attend(0)
    project(0)
    activate(0)
    spread(0)
    begin(1)
    attend(1)
    project(1)
    attend(2)
    project(2)
    activate(1)
    attend(3)
    project(3)
    spread(1)
    activate(2)
    spread(2)
    activate(3)
    spread(3)

    for f in range(2):
        for r in range(3):
            to_tm[f, r] = parts[2 * (1 - t) + f, 1 - t + r].astype(BF16)
    for f in range(4):
        to_edge[f] = parts[f, 3 * t].astype(BF16)
    sems = (o_send, o_recv)
    coeffs = [
        exchange(0, to_tm, from_tm, x_peers[0], sems),
        exchange(1, to_edge.at[frames], from_edge.at[0], x_peers[1], sems),
        exchange(2, to_edge.at[pl.ds(2 * (1 - t), 2)], from_edge.at[1], x_peers[2], sems),
    ]
    owned[...] = jnp.zeros(owned.shape, F32)
    for f in range(2):
        for r in range(3):
            owned[f, t + r] = parts[2 * t + f, 1 - t + r]
    for copy in sent + rows:
        copy.wait_send()
    for copy in coeffs:
        copy.wait_recv()
    which = jnp.where(s == t, 0, 1)
    for f in range(2):
        for r in range(3):
            owned[f, 1 - t + r] = owned[f, 1 - t + r] + from_tm[f, r].astype(F32)
        edge = from_edge[which, f].astype(F32)
        owned[f, 3 * (1 - s)] = owned[f, 3 * (1 - s)] + edge

    for f in range(2):
        for h in range(4):
            low, high = owned[f, h, 0:8, :], owned[f, h, 8:16, :]
            for i, value in enumerate((low + high, low - high)):
                at = pl.ds(32 * f + 2 * h + i, 4, stride=8)
                pixel_rows[0, at, :] = (value[0:4] + value[4:8]) * 0.5
                pixel_rows[1, at, :] = (value[0:4] - value[4:8]) * 0.5
    both = jnp.concatenate([pixel_rows[0], pixel_rows[1]], axis=1)
    big = both.astype(BF16)
    small = (both - big.astype(F32)).astype(BF16)
    image = dot(big, spread_cols[...]) + dot(small, spread_cols[...])
    for f in range(2):
        keep = jnp.where(2 * t + f < live, 1.0, 0.0).astype(F32)
        for colour in range(3):
            start = 32 * f + 8 * colour
            out[0, f, colour] = image[start : start + 8] * keep

    for copy in coeffs:
        copy.wait_send()


def solution(mesh):
    clips = mesh.shape["clip"]
    plane = 1 << (clips.bit_length() // 2)
    planes = clips // plane
    most = max(plane, planes)

    def body(
        gen_latent,
        frame_counts,
        owner_map,
        w_in,
        w_query,
        w_key,
        w_value,
        w_out,
        w_space,
        w_time,
        w_head,
    ):
        ch = w_query.shape[0]
        lat = jnp.swapaxes(gen_latent, -1, -2)[0]
        flat_in = w_in.reshape(144, ch)
        flat_space = w_space.reshape(9, ch, ch)
        vm = pltpu.VMEM
        dma = pltpu.SemaphoreType.DMA
        scratch = [
            vm((144, ch), BF16),
            vm((ch, ch), BF16),
            vm((ch, ch), BF16),
            vm((ch, ch), BF16),
            vm((ch, ch), BF16),
            vm((9, ch, ch), BF16),
            vm((3, ch, ch), BF16),
            vm((12, ch), BF16),
            pltpu.SMEM((clips,), jnp.int32),
            pltpu.SMEM((clips,), jnp.int32),
            vm((ch + 16, 144), BF16),
            vm((16, ch), BF16),
            vm((ch, ch), BF16),
            vm((ch + 16, ch), BF16),
            vm((48, ch), BF16),
            vm((3, 9, 16, ch), BF16),
            vm((PAIR, PAIR), BF16),
            vm((planes, 4, 16, WIDE), BF16),
            vm((plane, 4, 16, WIDE), BF16),
            vm((2, most, 4, 16, WIDE), BF16),
            vm((plane, 4, 16, WIDE), BF16),
            vm((planes, 4, 16, WIDE), BF16),
            vm((2, 4, 16, WIDE), BF16),
            vm((4, 4, 16, WIDE), BF16),
            vm((4, 144, PAIR), BF16),
            vm((4, ch + 16, PAIR), F32),
            vm((4, ch + 16, PAIR), F32),
            vm((4, ch, PAIR), BF16),
            vm((4, ch, PAIR), BF16),
            vm((4, ch, PAIR), BF16),
            vm((4, ch, PAIR), BF16),
            vm((4, 4, 16, WIDE), F32),
            vm((2, 3, 16, WIDE), BF16),
            vm((4, 16, WIDE), BF16),
            vm((2, 3, 16, WIDE), BF16),
            vm((2, 2, 16, WIDE), BF16),
            vm((2, 4, 16, WIDE), F32),
            vm((2, 64, WIDE), F32),
            dma((8,)),
            dma((4,)),
            dma((2, most)),
            dma((2, most)),
            dma((2, most)),
            dma((2, most)),
            dma((2, 3)),
            dma((2, 3)),
            dma((3,)),
            dma((3,)),
        ]
        hbm = pl.BlockSpec(memory_space=pltpu.HBM)
        return pl.pallas_call(
            functools.partial(kernel, plane, planes),
            out_shape=pltpu.VMEM((1, 2, 3, 8, 2 * WIDE), F32),
            in_specs=[hbm] * 11,
            out_specs=pl.BlockSpec(memory_space=pltpu.VMEM),
            scratch_shapes=scratch,
            compiler_params=pltpu.CompilerParams(
                collective_id=0, has_side_effects=True, vmem_limit_bytes=62 * 1024 * 1024
            ),
        )(
            owner_map,
            frame_counts,
            lat,
            flat_in,
            w_query,
            w_key,
            w_value,
            w_out,
            flat_space,
            w_time,
            w_head.T,
        )

    return jax.shard_map(
        body,
        mesh=mesh,
        in_specs=(P("clip", "tm", "space", None, None),) + (P(),) * 10,
        out_specs=P("clip", "tm", None, "space", None),
        check_vma=False,
    )
```

```python
import functools
import math

import jax
import jax.numpy as jnp
from jax import lax
from jax.experimental import pallas as pl
from jax.experimental.pallas import tpu as pltpu
from jax.sharding import PartitionSpec as P

EPS = 1e-06
MESH = pl.DeviceIdType.MESH
F32 = jnp.float32
BF16 = jnp.bfloat16
WIDE = 128
PAIR = 2 * WIDE


def dot(a, b):
    return jnp.dot(a, b, preferred_element_type=F32)


def dot_nt(a, b):
    return lax.dot_general(a, b, (((1,), (1,)), ((), ())), preferred_element_type=F32)


def kernel(
    plane,
    planes,
    owner_hbm,
    counts_hbm,
    lat,
    w_in,
    w_query,
    w_key,
    w_value,
    w_out,
    w_space,
    w_time,
    w_head,
    out,
    v_in,
    v_query,
    v_key,
    v_value,
    v_out,
    v_space,
    v_time,
    v_head,
    owner,
    counts,
    in_t,
    head16,
    qk_t,
    vo_t,
    taps,
    eff,
    spread_cols,
    gat_a,
    gat_b,
    p_buf,
    got_a,
    got_b,
    quarter,
    panel,
    patches,
    first,
    second,
    normal,
    query,
    mixed,
    active,
    parts,
    to_tm,
    to_edge,
    from_tm,
    from_edge,
    owned,
    pixel_rows,
    w_sem,
    own_sem,
    g_send,
    g_recv,
    p_send,
    p_recv,
    x_send,
    x_recv,
    o_send,
    o_recv,
):
    ch = v_query.shape[0]
    me = lax.axis_index("clip")
    s = lax.axis_index("space")
    t = lax.axis_index("tm")
    m = lax.rem(me, plane)
    z = me // plane
    base = z * plane
    gat = (gat_a, gat_b)
    got = (got_a, got_b)

    loads = [
        pltpu.make_async_copy(src, dst, w_sem.at[i])
        for i, (src, dst) in enumerate(
            (
                (w_key, v_key),
                (w_query, v_query),
                (w_value, v_value),
                (w_out, v_out),
                (w_head, v_head),
                (w_in, v_in),
                (w_time, v_time),
                (w_space, v_space),
            )
        )
    ]
    l_key, l_query, l_value, l_out, l_head, l_in, l_time, l_space = loads

    def others(count, place):
        return [i + (i + count - place) // count for i in range(count - 1)]

    def plane_peer(q):
        return (base + q, s, t)

    def column_peer(q):
        return (q * plane + m, s, t)

    x_peers = [(me, s, 1 - t), (me, 1 - s, t), (me, 1 - s, 1 - t)]
    everyone = [column_peer(q) for q in others(planes, z)] + x_peers
    everyone += [plane_peer(q) for q in others(plane, m)]
    barrier = pltpu.get_barrier_semaphore()
    for peer in everyone:
        pl.semaphore_signal(barrier, inc=1, device_id=peer, device_id_type=MESH)
    ways = ((planes, column_peer, z), (plane, plane_peer, m))
    own = [
        pltpu.make_async_copy(lat.at[c], gat[c].at[ways[c][2]], own_sem.at[c]) for c in range(2)
    ]
    tables = [
        pltpu.make_async_copy(owner_hbm, owner, own_sem.at[2]),
        pltpu.make_async_copy(counts_hbm, counts, own_sem.at[3]),
    ]
    for copy in own + tables:
        copy.start()

    def start_loads():
        for load in loads:
            load.start()

    def products():
        l_key.wait()
        l_query.wait()
        qk_t[...] = dot_nt(v_key[...], v_query[...]).astype(BF16)
        l_value.wait()
        l_out.wait()
        vo_t[0:ch, :] = dot(v_value[...], v_out[...]).T.astype(BF16)
        l_head.wait()
        wide = v_head[...].astype(F32)
        gap = jnp.zeros((1, ch), F32)
        head16[...] = jnp.concatenate(
            [wide[0:3], gap, wide[3:6], gap, wide[6:9], gap, wide[9:12], gap], axis=0
        ).astype(BF16)
        l_time.wait()
        for k in range(3):
            taps[16 * k : 16 * k + 16, :] = dot_nt(head16[...], v_time[2 - k]).astype(BF16)

        l_in.wait()
        in_t[0:ch, :] = v_in[...].astype(F32).T.astype(BF16)
        in_t[ch : ch + 16, :] = dot_nt(head16[...], v_in[...]).astype(BF16)
        vo_t[ch : ch + 16, :] = dot(head16[...], vo_t[0:ch, :]).astype(BF16)
        l_space.wait()

        def fold(i):
            got = dot_nt(taps[...], v_space[i]).astype(BF16)
            for k in range(3):
                eff[k, i] = got[16 * k : 16 * k + 16]

        for i in range(9):
            fold(i)

        r_id = lax.broadcasted_iota(jnp.int32, (PAIR, PAIR), 0)
        c_id = lax.broadcasted_iota(jnp.int32, (PAIR, PAIR), 1)
        goal = jnp.where(r_id < WIDE, 2 * r_id, 2 * (r_id - WIDE) + 1)
        spread_cols[...] = jnp.where(goal == c_id, 1.0, 0.0).astype(BF16)
        parts[...] = jnp.zeros(parts.shape, F32)

    early = z + lax.rem(m, 2) + m // 2 < planes // 2

    last = jnp.logical_and(z >= planes // 2, m >= plane // 2)
    pl.when(jnp.logical_not(last))(start_loads)
    pl.when(early)(products)

    for copy in own:
        copy.wait()
    pl.semaphore_wait(barrier, len(everyone))

    def send(i, src, dst, sems, place, device):
        copy = pltpu.make_async_remote_copy(
            src_ref=src,
            dst_ref=dst,
            send_sem=sems[0].at[i],
            recv_sem=sems[1].at[place],
            device_id=device,
            device_id_type=MESH,
        )
        copy.start()
        return copy

    def arrive(dst, sems, place, device):
        pltpu.make_async_remote_copy(
            src_ref=dst,
            dst_ref=dst,
            send_sem=sems[0].at[0],
            recv_sem=sems[1].at[place],
            device_id=device,
            device_id_type=MESH,
        ).wait_recv()

    sent = []
    for c in range(2):
        count, peer, place = ways[c]
        sems = (g_send.at[c], g_recv.at[c])
        block = gat[c].at[place]
        for i, q in enumerate(others(count, place)):
            sent.append(send(i, block, block, sems, place, peer(q)))

    for copy in tables:
        copy.wait()

    def pick(c, q):
        found = jnp.int32(0)
        for i in range(ways[c][0]):
            here, goal = (i * plane + m, base + q) if c == 0 else (base + i, q * plane + m)
            found = jnp.where(owner[here] == goal, jnp.int32(i), found)
        return found

    for c in (1, 0):
        count, peer, place = ways[c]
        sems = (g_send.at[c], g_recv.at[c])
        for q in others(count, place):
            arrive(gat[c].at[q], sems, q, peer(q))
        count, peer, place = ways[1 - c]
        sems = (p_send.at[c], p_recv.at[c])
        for i, q in enumerate(others(count, place)):
            p_buf[c, i] = gat[c][pick(c, q)]
            sent.append(send(i, p_buf.at[c, i], got[c].at[place], sems, place, peer(q)))
        got[c][place] = gat[c][pick(c, place)]

    pl.when(last)(start_loads)

    def scan(g, carry):
        from_a, from_b, live = carry
        here = owner[g] == me
        return (
            jnp.where(here, lax.rem(g, plane), from_a),
            jnp.where(here, g // plane, from_b),
            jnp.where(here, counts[g], live),
        )

    from_a, from_b, live = lax.fori_loop(0, plane * planes, scan, (jnp.int32(0),) * 3, unroll=8)

    pl.when(jnp.logical_not(early))(products)

    for c in range(2):
        count, peer, place = ways[1 - c]
        for q in others(count, place):
            arrive(got[c].at[q], (p_send.at[c], p_recv.at[c]), q, peer(q))
    quarter[0] = got_a[from_a]
    quarter[1] = got_b[from_b]

    def exchange(i, src, dst, peer, sems):
        copy = pltpu.make_async_remote_copy(
            src_ref=src,
            dst_ref=dst,
            send_sem=sems[0].at[i],
            recv_sem=sems[1].at[i],
            device_id=peer,
            device_id_type=MESH,
        )
        copy.start()
        return copy

    frames = pl.ds(2 * t, 2)
    sems = (x_send, x_recv)
    rows = [
        exchange(0, quarter.at[:, pl.ds(1 - t, 3)], panel.at[frames, pl.ds(t, 3)], x_peers[0], sems),
        exchange(1, quarter.at[:, 3 * (1 - s)], panel.at[frames, 3 * t], x_peers[1], sems),
        exchange(2, quarter.at[:, 3 * (1 - s)], panel.at[frames, 3 * (1 - t)], x_peers[2], sems),
    ]
    for f in range(2):
        for r in range(3):
            panel[2 * t + f, 1 - t + r] = quarter[f, t + r]

    for copy in rows:
        copy.wait_recv()

    lane = lax.broadcasted_iota(jnp.int32, (16, WIDE), 1)
    top = jnp.logical_not(jnp.logical_and(s == 0, t == 0))
    bottom = jnp.logical_not(jnp.logical_and(s == 1, t == 1))
    for f in range(4):
        for r in range(4):
            tile = panel[f, r].astype(F32)
            if r == 0:
                tile = jnp.where(top, tile, 0.0)
            if r == 3:
                tile = jnp.where(bottom, tile, 0.0)
            left = jnp.where(lane == 0, 0.0, pltpu.roll(tile, 1, 1))
            right = jnp.where(lane == WIDE - 1, 0.0, pltpu.roll(tile, WIDE - 1, 1))
            for b, value in enumerate((left, tile, right)):
                value = value.astype(BF16)
                for a in range(3):
                    row = r - a
                    if row in (0, 1):
                        start = 16 * (3 * a + b)
                        patches[f, start : start + 16, row * WIDE : (row + 1) * WIDE] = value

    def inverse_rms(square):
        return lax.rsqrt(jnp.sum(square, axis=0, keepdims=True) / ch + EPS)

    tiles = [slice(c, c + 16) for c in range(0, ch, 16)]

    for f in range(4):
        first[f] = dot(in_t[...], patches[f])

    def make_query(f):
        square = jnp.zeros((16, PAIR), F32)
        for c in tiles:
            x = first[f, c, :]
            square = square + x * x
        scale = inverse_rms(square)
        for c in tiles:
            normal[f, c, :] = (first[f, c, :] * scale).astype(BF16)
        query[f] = dot(qk_t[...], normal[f]).astype(BF16)

    def attend(f):
        accs = [jnp.zeros((16, PAIR), F32)] * (f + 1)
        for c in range(0, ch, 64):
            for g in range(f + 1):
                p = [
                    query[f, i : i + 16, :] * normal[g, i : i + 16, :]
                    for i in range(c, c + 64, 16)
                ]
                accs[g] = accs[g] + ((p[0] + p[1]) + (p[2] + p[3])).astype(F32)
        scores = [jnp.sum(acc, axis=0, keepdims=True) * (1.0 / math.sqrt(ch)) for acc in accs]
        highest = functools.reduce(jnp.maximum, scores)
        weights = [jnp.exp(x - highest) for x in scores]
        norm = 1.0 / functools.reduce(jnp.add, weights)
        weights = [jnp.broadcast_to(w * norm, (16, PAIR)).astype(BF16) for w in weights]
        for c in tiles:
            mixed[f, c, :] = functools.reduce(
                jnp.add, [w * normal[g, c, :] for g, w in enumerate(weights)]
            )

    def project(f):
        second[f] = dot(vo_t[...], mixed[f])

    def activate(f):
        square = jnp.zeros((16, PAIR), F32)
        for c in tiles:
            x = first[f, c, :] + second[f, c, :]
            second[f, c, :] = x
            square = square + x * x
        scale = inverse_rms(square) * 0.5
        for c in tiles:
            x = second[f, c, :] * scale
            active[f, c, :] = (x + x * jnp.tanh(x)).astype(BF16)
        for row in range(2):
            here = slice(row * WIDE, (row + 1) * WIDE)
            head = first[f, ch : ch + 16, here] + second[f, ch : ch + 16, here]
            parts[f, row + 1] = parts[f, row + 1] + head

    def spread(f):
        steps = min(3, 4 - f)
        wide = dot(eff[0:steps].reshape(144 * steps, ch), active[f])
        for k in range(steps):
            for r in range(4):
                sides = []
                for b in range(3):
                    pieces = []
                    for row in range(2):
                        a = row + 2 - r
                        if 0 <= a < 3:
                            start = 144 * k + 16 * (3 * a + b)
                            here = slice(row * WIDE, (row + 1) * WIDE)
                            pieces.append(wide[start : start + 16, here])
                    sides.append(functools.reduce(jnp.add, pieces))
                left = jnp.where(lane == 0, 0.0, pltpu.roll(sides[0], 1, 1))
                right = jnp.where(lane == WIDE - 1, 0.0, pltpu.roll(sides[2], WIDE - 1, 1))
                parts[f + k, r] = parts[f + k, r] + (sides[1] + (left + right))

    for f in range(4):
        make_query(f)
    attend(0)
    project(0)
    attend(1)
    project(1)
    activate(0)
    attend(2)
    project(2)
    spread(0)
    activate(1)
    attend(3)
    project(3)
    spread(1)
    activate(2)
    spread(2)
    activate(3)
    spread(3)

    for f in range(2):
        for r in range(3):
            to_tm[f, r] = parts[2 * (1 - t) + f, 1 - t + r].astype(BF16)
    for f in range(4):
        to_edge[f] = parts[f, 3 * t].astype(BF16)
    sems = (o_send, o_recv)
    coeffs = [
        exchange(0, to_tm, from_tm, x_peers[0], sems),
        exchange(1, to_edge.at[frames], from_edge.at[0], x_peers[1], sems),
        exchange(2, to_edge.at[pl.ds(2 * (1 - t), 2)], from_edge.at[1], x_peers[2], sems),
    ]
    owned[...] = jnp.zeros(owned.shape, F32)
    for f in range(2):
        for r in range(3):
            owned[f, t + r] = parts[2 * t + f, 1 - t + r]
    for copy in sent + rows:
        copy.wait_send()
    for copy in coeffs:
        copy.wait_recv()
    which = jnp.where(s == t, 0, 1)
    for f in range(2):
        for r in range(3):
            owned[f, 1 - t + r] = owned[f, 1 - t + r] + from_tm[f, r].astype(F32)
        edge = from_edge[which, f].astype(F32)
        owned[f, 3 * (1 - s)] = owned[f, 3 * (1 - s)] + edge

    for f in range(2):
        for h in range(4):
            low, high = owned[f, h, 0:8, :], owned[f, h, 8:16, :]
            for i, value in enumerate((low + high, low - high)):
                at = pl.ds(32 * f + 2 * h + i, 4, stride=8)
                pixel_rows[0, at, :] = (value[0:4] + value[4:8]) * 0.5
                pixel_rows[1, at, :] = (value[0:4] - value[4:8]) * 0.5
    both = jnp.concatenate([pixel_rows[0], pixel_rows[1]], axis=1)
    big = both.astype(BF16)
    small = (both - big.astype(F32)).astype(BF16)
    image = dot(big, spread_cols[...]) + dot(small, spread_cols[...])
    for f in range(2):
        keep = jnp.where(2 * t + f < live, 1.0, 0.0).astype(F32)
        for colour in range(3):
            start = 32 * f + 8 * colour
            out[0, f, colour] = image[start : start + 8] * keep

    for copy in coeffs:
        copy.wait_send()


def solution(mesh):
    clips = mesh.shape["clip"]
    plane = 1 << (clips.bit_length() // 2)
    planes = clips // plane
    most = max(plane, planes)

    def body(
        gen_latent,
        frame_counts,
        owner_map,
        w_in,
        w_query,
        w_key,
        w_value,
        w_out,
        w_space,
        w_time,
        w_head,
    ):
        ch = w_query.shape[0]
        lat = jnp.swapaxes(gen_latent, -1, -2)[0]
        flat_in = w_in.reshape(144, ch)
        flat_space = w_space.reshape(9, ch, ch)
        vm = pltpu.VMEM
        dma = pltpu.SemaphoreType.DMA
        scratch = [
            vm((144, ch), BF16),
            vm((ch, ch), BF16),
            vm((ch, ch), BF16),
            vm((ch, ch), BF16),
            vm((ch, ch), BF16),
            vm((9, ch, ch), BF16),
            vm((3, ch, ch), BF16),
            vm((12, ch), BF16),
            pltpu.SMEM((clips,), jnp.int32),
            pltpu.SMEM((clips,), jnp.int32),
            vm((ch + 16, 144), BF16),
            vm((16, ch), BF16),
            vm((ch, ch), BF16),
            vm((ch + 16, ch), BF16),
            vm((48, ch), BF16),
            vm((3, 9, 16, ch), BF16),
            vm((PAIR, PAIR), BF16),
            vm((planes, 4, 16, WIDE), BF16),
            vm((plane, 4, 16, WIDE), BF16),
            vm((2, most, 4, 16, WIDE), BF16),
            vm((plane, 4, 16, WIDE), BF16),
            vm((planes, 4, 16, WIDE), BF16),
            vm((2, 4, 16, WIDE), BF16),
            vm((4, 4, 16, WIDE), BF16),
            vm((4, 144, PAIR), BF16),
            vm((4, ch + 16, PAIR), F32),
            vm((4, ch + 16, PAIR), F32),
            vm((4, ch, PAIR), BF16),
            vm((4, ch, PAIR), BF16),
            vm((4, ch, PAIR), BF16),
            vm((4, ch, PAIR), BF16),
            vm((4, 4, 16, WIDE), F32),
            vm((2, 3, 16, WIDE), BF16),
            vm((4, 16, WIDE), BF16),
            vm((2, 3, 16, WIDE), BF16),
            vm((2, 2, 16, WIDE), BF16),
            vm((2, 4, 16, WIDE), F32),
            vm((2, 64, WIDE), F32),
            dma((8,)),
            dma((4,)),
            dma((2, most)),
            dma((2, most)),
            dma((2, most)),
            dma((2, most)),
            dma((3,)),
            dma((3,)),
            dma((3,)),
            dma((3,)),
        ]
        hbm = pl.BlockSpec(memory_space=pltpu.HBM)
        return pl.pallas_call(
            functools.partial(kernel, plane, planes),
            out_shape=pltpu.VMEM((1, 2, 3, 8, 2 * WIDE), F32),
            in_specs=[hbm] * 11,
            out_specs=pl.BlockSpec(memory_space=pltpu.VMEM),
            scratch_shapes=scratch,
            compiler_params=pltpu.CompilerParams(
                collective_id=0, has_side_effects=True, vmem_limit_bytes=62 * 1024 * 1024
            ),
        )(
            owner_map,
            frame_counts,
            lat,
            flat_in,
            w_query,
            w_key,
            w_value,
            w_out,
            flat_space,
            w_time,
            w_head.T,
        )

    return jax.shard_map(
        body,
        mesh=mesh,
        in_specs=(P("clip", "tm", "space", None, None),) + (P(),) * 10,
        out_specs=P("clip", "tm", None, "space", None),
        check_vma=False,
    )
```
